256 devices in a mesh: row: 32 (over y, x, core), col: 8 (over z).
Axes of the slice: x: 4, y: 4, z: 8, core: 2. Of those that a mesh axis runs over, the one named last changes fastest.
Arguments:
- probes: float32 [8, 2048, 2048], P(None, 'row', 'col'), may hold values from -6 to 6
- kappa_sq: float32 [2048, 2048], P('row', 'col'), may hold values from 0.05 to 1
- conduct: float32 [2048, 2048], P('row', 'col'), may hold values from 0.05 to 0.25
- inv_mass: float32 [2048, 2048], P('row', 'col'), may hold values from 0.5 to 2
- spai: bfloat16 [25, 2048, 2048], P(None, 'row', 'col'), may hold values from -0.04 to 2, as said below
- sea_mask: int32 [2048, 2048], P('row', 'col'), may hold values 0 or 1
Outputs:
- solution_field: float32 [8, 2048, 2048], P(None, 'row', 'col')
- residual: float32 [8, 2048, 2048], P(None, 'row', 'col')
The draws below stay inside these ranges and needn't reach their ends.
Inputs may be any that keep to these rules, and one draw needn't show every extreme that they name: `spai`: channel 12 (no offset) lies in 1 to 2, every other channel in -0.04 to 0.04.
All inputs are finite; a program needn't handle non-finite values. No bound on the sum of `sea_mask` on one device may be relied on, other than what follows from the above.
Results may differ from the reference program's by a relative error of at most 0.0003.
Values may be sent and summed in bfloat16 or wider, within the bound.
A program may use at most 64 MiB of HBM per device.

```python
import math
import jax
import jax.numpy as jnp
from jax import lax

PROBES = 8
ITERS = 2
NX = 2048
NY = 2048


def draw_spai(key, part):
    key_off, key_centre = jax.random.split(jax.random.fold_in(key, 17))
    off = jax.random.uniform(key_off, (25, NX, NY), jnp.float32, -0.039, 0.039)
    centre = jax.random.uniform(jax.random.fold_in(key_centre, 3), (NX, NY), jnp.float32, 1.0, 2.0)
    channel = jnp.arange(25)[:, None, None]
    return jnp.where(channel == 12, centre[None], off).astype(jnp.bfloat16)


def place_ends(result, stream_key, smallest, high):
    spot = [jax.random.randint(jax.random.fold_in(stream_key, axis), (), 0, length) for axis, length in enumerate(result.shape)]
    longest = result.shape.index(max(result.shape))
    neighbour = spot[:longest] + [(spot[longest] + 1) % result.shape[longest]] + spot[longest + 1:]
    return result.at[tuple(spot)].set(smallest).at[tuple(neighbour)].set(high)


def levels(stream_key, dims, shards, smallest, top_value):
    def one(position, blocks):
        heights = jax.random.uniform(jax.random.fold_in(jax.random.fold_in(stream_key, 6), position), (blocks,), jnp.float32, smallest / len(shards), top_value / len(shards))
        return jnp.repeat(jnp.exp(heights), dims[position] // blocks).reshape((-1,) + (1,) * (len(dims) - position - 1))

    factor_of = one(*shards[0])
    for cut in shards[1:]:
        factor_of = factor_of * one(*cut)
    return factor_of


def noise(rng, dims, spread, bound, cuts=(), dtype=jnp.bfloat16):
    result = jax.random.normal(rng, dims, jnp.float32) * spread
    if len(cuts) > 0:
        result = levels(rng, dims, cuts, -0.22, 0.18) * result
    return jnp.clip(result, min=-bound, max=bound).astype(dtype)


def setup_inputs(seed: int = 0) -> dict:
    seeds = jax.random.split(jax.random.key(seed), 7)
    return {
        "probes": noise(seeds[0], (PROBES, NX, NY), 1.0, 6.0, ((1, 32), (2, 8)), jnp.float32),
        "kappa_sq": jnp.clip(jnp.exp(math.log(1.0) - 2.9957323 * jax.random.uniform(seeds[1], (NX, NY), jnp.float32) ** levels(seeds[1], (NX, NY), ((0, 32), (1, 8)), -0.2, 0.2)), 0.05, 1.0),
        "conduct": jnp.clip(jnp.exp(math.log(0.25) - 1.609438 * jax.random.uniform(seeds[2], (NX, NY), jnp.float32) ** levels(seeds[2], (NX, NY), ((0, 32), (1, 8)), -0.2, 0.2)), 0.05, 0.25),
        "inv_mass": jnp.clip(jnp.exp(math.log(2.0) - 1.3862944 * jax.random.uniform(seeds[3], (NX, NY), jnp.float32) ** levels(seeds[3], (NX, NY), ((0, 32), (1, 8)), -0.2, 0.2)), 0.5, 2.0),
        "spai": draw_spai(jax.random.fold_in(seeds[6], 71), 0),
        "sea_mask": place_ends((jax.random.randint(seeds[5], (NX, NY), 0, 5) < 4).astype(jnp.int32), jax.random.fold_in(seeds[5], 1), 0, 1),
    }


def laplace(padded_field, kap, padded_cond):
    centre = padded_field[:, 1:-1, 1:-1]
    cond_centre = padded_cond[1:-1, 1:-1]
    total = kap * centre
    shifts = [(slice(0, -2), slice(1, -1)), (slice(2, None), slice(1, -1)), (slice(1, -1), slice(0, -2)), (slice(1, -1), slice(2, None))]
    for first, second in shifts:
        cond_near = padded_cond[first, second]
        field_near = padded_field[:, first, second]
        total = total + 0.5 * (cond_centre + cond_near) * (centre - field_near)
    return total

def symmetric(weights, padded_weights, nrow, ncol):
    rows_out = []
    for offset in range(25):
        shift_a = offset // 5 - 2
        shift_b = offset % 5 - 2
        mirror = padded_weights[24 - offset, 2 + shift_a:2 + shift_a + nrow, 2 + shift_b:2 + shift_b + ncol]
        rows_out.append(0.5 * (weights[offset] + mirror))
    return jnp.stack(rows_out)

def combine(sym, padded_field, nrow, ncol):
    total = jnp.zeros((padded_field.shape[0], nrow, ncol), jnp.float32)
    for offset in range(25):
        shift_a = offset // 5 - 2
        shift_b = offset % 5 - 2
        total = total + sym[offset][None] * padded_field[:, 2 + shift_a:2 + shift_a + nrow, 2 + shift_b:2 + shift_b + ncol]
    return total

def gram(left, right):
    return jnp.einsum('kij,lij->kl', left, right, precision=lax.Precision.HIGHEST)

def mix(coef, field):
    return jnp.einsum('kl,kij->lij', coef, field, precision=lax.Precision.HIGHEST)

def solve_small(matrix, rhs):
    matrix = 0.5 * (matrix + matrix.T)
    factor = jnp.linalg.cholesky(matrix)
    return jax.scipy.linalg.cho_solve((factor, True), rhs)

def reference(probes, kappa_sq, conduct, inv_mass, spai, sea_mask):
    sea = sea_mask.astype(jnp.float32)
    padded_cond = jnp.pad(conduct, 1)
    weights = spai.astype(jnp.float32)
    sym = symmetric(weights, jnp.pad(weights, ((0, 0), (2, 2), (2, 2))), NX, NY)

    def apply_op(field):
        masked = sea[None] * field
        inner = laplace(jnp.pad(masked, ((0, 0), (1, 1), (1, 1))), kappa_sq, padded_cond)
        scaled = inv_mass[None] * inner
        outer = laplace(jnp.pad(scaled, ((0, 0), (1, 1), (1, 1))), kappa_sq, padded_cond)
        return sea[None] * outer + (1.0 - sea[None]) * field

    def precond(field):
        return combine(sym, jnp.pad(field, ((0, 0), (2, 2), (2, 2))), NX, NY)
    solution_field = jnp.zeros_like(probes)
    residual = probes
    zvec = precond(residual)
    direction = zvec
    gamma = gram(residual, zvec)
    for step in range(ITERS):
        image = apply_op(direction)
        alpha = solve_small(gram(direction, image), gamma)
        solution_field = solution_field + mix(alpha, direction)
        residual = residual - mix(alpha, image)
        if step + 1 < ITERS:
            zvec = precond(residual)
            gamma_new = gram(residual, zvec)
            beta = solve_small(gamma, gamma_new)
            direction = zvec + mix(beta, direction)
            gamma = gamma_new
    return (solution_field, residual)
```

```python
import functools

import jax
import jax.numpy as jnp
from jax import lax
from jax.experimental import pallas as pl
from jax.experimental.pallas import tpu as pltpu
from jax.sharding import PartitionSpec as P

MESH = pl.DeviceIdType.MESH
PROBES = 8
LANES = 128
HALO = 8
OFF = 16
OFFSETS = [(o // 5 - 2, o % 5 - 2) for o in range(25)]


def tile_shift(tiles, place, step, lane):
    if step == 0:
        return tiles[place]
    count = len(tiles)
    here = pltpu.roll(tiles[place], (-step) % LANES, axis=1)
    if step > 0:
        there = pltpu.roll(tiles[(place + 1) % count], (-step) % LANES, axis=1)
        return jnp.where(lane < LANES - step, here, there)
    there = pltpu.roll(tiles[(place - 1) % count], (-step) % LANES, axis=1)
    return jnp.where(lane >= -step, here, there)


def ring_shifts(tiles, step, lane):
    if step == 0:
        return list(tiles)
    count = len(tiles)
    rolled = [pltpu.roll(tile, (-step) % LANES, axis=1) for tile in tiles]
    if step > 0:
        return [jnp.where(lane < LANES - step, rolled[u], rolled[(u + 1) % count]) for u in range(count)]
    return [jnp.where(lane >= -step, rolled[u], rolled[(u - 1) % count]) for u in range(count)]


def splats(matrix, first):
    out = [[None] * 8 for _ in range(8)]
    for col in range(8):
        wide = jnp.broadcast_to(matrix[:, first + col : first + col + 1], (8, LANES))
        for row in range(8):
            out[row][col] = jnp.broadcast_to(wide[row : row + 1, :], (8, LANES))
    return out


def rows_of(matrix):
    return [jnp.broadcast_to(matrix[k : k + 1, :], (8, LANES)) for k in range(8)]


def stack_rows(rows, sub):
    out = rows[0]
    for k in range(1, 8):
        out = jnp.where(sub == k, rows[k], out)
    return out


def product(left, rows):
    out = []
    for i in range(8):
        total = left[i][0] * rows[0]
        for j in range(1, 8):
            total = total + left[i][j] * rows[j]
        out.append(total)
    return out


def product_t(left, rows):
    return product([[left[j][i] for j in range(8)] for i in range(8)], rows)


def factor(entries):
    a = [list(r) for r in entries]
    mult = [[None] * 8 for _ in range(8)]
    inverse = []
    for j in range(8):
        inv = 1.0 / a[j][j]
        inverse.append(inv)
        for k in range(j + 1, 8):
            mult[k][j] = a[j][k] * inv
            for m in range(k, 8):
                a[k][m] = a[k][m] - mult[k][j] * a[j][m]
    return mult, inverse


def substitute(fact, rows):
    mult, inverse = fact
    y = list(rows)
    for j in range(8):
        for k in range(j + 1, 8):
            y[k] = y[k] - mult[k][j] * y[j]
    y = [y[j] * inverse[j] for j in range(8)]
    for j in range(7, -1, -1):
        for k in range(j):
            y[k] = y[k] - mult[j][k] * y[j]
    return y


def kernel(
    nrow, ncol, rows_n, cols_n,
    probes, kappa, conduct, inv_mass, spai, sea,
    x_out, r_out,
    rbuf, zbuf, wbuf, ybuf, tbuf, sraw, sfull, symp, cbuf, lap,
    pland, cland, seal, seaown, cpack, spack, crecv, srecv,
    grams1, grams2, coef, xs, rs,
    lsem, ssem, rsem, s1, r1, s2, r2, osem,
):
    nu = ncol // LANES
    nt = nu + 1
    row = lax.axis_index("row")
    col = lax.axis_index("col")
    core = row % 2
    pair = row // 2
    group1 = 2 * cols_n
    group2 = rows_n // 2
    up, down = (row + rows_n - 1) % rows_n, (row + 1) % rows_n
    left, right = (col + cols_n - 1) % cols_n, (col + 1) % cols_n
    mine1 = core * cols_n + col

    partners1 = []
    for d in range(1, group1):
        q = (mine1 + d) % group1
        partners1.append((row - core + q // cols_n, q % cols_n))
    partners2 = []
    for d in range(1, group2):
        q = (pair + d) % group2
        partners2.append((2 * q + core, col))
    around = [(up, left), (up, col), (up, right), (row, left), (row, right), (down, left), (down, col), (down, right)]

    barrier = pltpu.get_barrier_semaphore()
    for who in around + partners1 + partners2:
        pl.semaphore_signal(barrier, inc=1, device_id=who, device_id_type=MESH)

    local = []
    local.append(pltpu.make_async_copy(spai, sraw.at[:, pl.ds(OFF, nrow), :], lsem.at[0]))
    for u in range(nu):
        local.append(pltpu.make_async_copy(
            probes.at[:, :, pl.ds(u * LANES, LANES)], rbuf.at[u, :, pl.ds(OFF, nrow), :], lsem.at[1 + u]))
    for k, field in enumerate((kappa, conduct, inv_mass)):
        for u in range(nu):
            local.append(pltpu.make_async_copy(
                field.at[:, pl.ds(u * LANES, LANES)], cbuf.at[k, u, pl.ds(OFF, nrow), :], lsem.at[1 + nu + k * nu + u]))
    local.append(pltpu.make_async_copy(sea, seaown, lsem.at[1 + 4 * nu]))
    for copy in local:
        copy.start()

    pl.semaphore_wait(barrier, len(around) + len(partners1) + len(partners2))

    def remote(index, src, dst, who):
        return pltpu.make_async_remote_copy(
            src_ref=src, dst_ref=dst, send_sem=ssem.at[index], recv_sem=rsem.at[index],
            device_id=who, device_id_type=MESH)

    row_copies = []
    for side, who in ((0, down), (1, up)):
        first = nrow - HALO if side == 0 else 0
        first16 = nrow - OFF if side == 0 else 0
        land16 = 0 if side == 0 else OFF + nrow
        base = 6 * side
        row_copies.append(remote(base, spai.at[:, pl.ds(first16, OFF), :], sraw.at[:, pl.ds(land16, OFF), :], (who, col)))
        row_copies.append(remote(base + 1, probes.at[:, pl.ds(first, HALO), :], pland.at[side], (who, col)))
        for k, field in enumerate((kappa, conduct, inv_mass)):
            row_copies.append(remote(base + 2 + k, field.at[pl.ds(first, HALO), :], cland.at[side, k], (who, col)))
        row_copies.append(remote(base + 5, sea.at[pl.ds(first, HALO), :], seal.at[side], (who, col)))
    for copy in row_copies:
        copy.start()

    for copy in local:
        copy.wait()

    lane = lax.broadcasted_iota(jnp.int32, (8, LANES), 1)
    sub = lax.broadcasted_iota(jnp.int32, (8, LANES), 0)
    lane16 = lax.broadcasted_iota(jnp.int32, (16, LANES), 1)

    def sea_body(t, carry):
        for u in range(nu):
            rows = pl.ds(pl.multiple_of(8 * t, 8), 8)
            dst = pl.ds(pl.multiple_of(OFF + 8 * t, 8), 8)
            cbuf[3, u, dst, :] = seaown[rows, u * LANES : (u + 1) * LANES].astype(jnp.float32)
        return carry
    lax.fori_loop(0, nrow // 8, sea_body, 0)

    def pack_body(t, carry):
        src = pl.ds(pl.multiple_of(OFF + 8 * t, 8), 8)
        dst = pl.ds(pl.multiple_of(8 * t, 8), 8)
        group = lane // HALO
        for side, u in ((0, 0), (1, nu - 1)):
            total = jnp.zeros((8, LANES), jnp.float32)
            for k in range(12):
                item = rbuf[u, k, src, :] if k < 8 else cbuf[k - 8, u, src, :]
                shift = (HALO * k + (0 if side == 0 else HALO)) % LANES
                moved = pltpu.roll(item, shift, axis=1) if shift else item
                total = jnp.where(group == k, moved, total)
            cpack[side, dst, :] = total
        return carry
    lax.fori_loop(0, nrow // 8, pack_body, 0)

    def spack_body(t, carry):
        src = pl.ds(pl.multiple_of(OFF + 16 * t, 16), 16)
        dst = pl.ds(pl.multiple_of(16 * t, 16), 16)
        group = lane16 // HALO
        for o in range(25):
            tiles = []
            for u in range(nu):
                tile = sraw[o, src, u * LANES : (u + 1) * LANES].astype(jnp.float32)
                sfull[u, o, src, :] = tile
                tiles.append(tile)
            if o % 16 == 0:
                totals = [jnp.zeros((16, LANES), jnp.float32)] * 2
            for side, u in ((0, 0), (1, nu - 1)):
                shift = (HALO * o + (0 if side == 0 else HALO)) % LANES
                moved = pltpu.roll(tiles[u], shift, axis=1) if shift else tiles[u]
                totals[side] = jnp.where(group == o % 16, moved, totals[side])
            if o % 16 == 15 or o == 24:
                part = o // 16
                for side in range(2):
                    spack[side, dst, part * LANES : (part + 1) * LANES] = totals[side].astype(jnp.bfloat16)
        return carry
    lax.fori_loop(0, nrow // 16, spack_body, 0)

    col_copies = []
    for side, who in ((0, left), (1, right)):
        to = 1 - side
        base = 12 + 6 * side
        col_copies += [
            remote(base, spack.at[side], srecv.at[to, pl.ds(OFF, nrow), :], (row, who)),
            remote(base + 1, cpack.at[side], crecv.at[to, pl.ds(HALO, nrow), :], (row, who)),
            remote(base + 2, spack.at[side, pl.ds(0, OFF), :], srecv.at[to, pl.ds(OFF + nrow, OFF), :], (up, who)),
            remote(base + 3, cpack.at[side, pl.ds(0, HALO), :], crecv.at[to, pl.ds(HALO + nrow, HALO), :], (up, who)),
            remote(base + 4, spack.at[side, pl.ds(nrow - OFF, OFF), :], srecv.at[to, pl.ds(0, OFF), :], (down, who)),
            remote(base + 5, cpack.at[side, pl.ds(nrow - HALO, HALO), :], crecv.at[to, pl.ds(0, HALO), :], (down, who)),
        ]
    for copy in col_copies:
        copy.start()

    one = jnp.float32(1.0)
    zero = jnp.float32(0.0)
    has_up = jnp.where(row > 0, one, zero)
    has_down = jnp.where(row < rows_n - 1, one, zero)
    has_left = jnp.where(col > 0, one, zero)
    has_right = jnp.where(col < cols_n - 1, one, zero)

    for copy in row_copies:
        copy.wait()
    for side, keep, at in ((0, has_up, OFF - HALO), (1, has_down, OFF + nrow)):
        for u in range(nu):
            cols = slice(u * LANES, (u + 1) * LANES)
            for p in range(PROBES):
                rbuf[u, p, at : at + 8, :] = pland[side, p, :, cols] * keep
            for k in range(3):
                cbuf[k, u, at : at + 8, :] = cland[side, k, :, cols] * keep
            cbuf[3, u, at : at + 8, :] = seal[side, :, cols].astype(jnp.float32) * keep
        start = 0 if side == 0 else OFF + nrow

        def sland_body(o, carry, start=start, keep=keep):
            for u in range(nu):
                sfull[u, o, start : start + 16, :] = (
                    sraw[o, start : start + 16, u * LANES : (u + 1) * LANES].astype(jnp.float32) * keep)
            return carry
        lax.fori_loop(0, 25, sland_body, 0)

    for copy in col_copies:
        copy.wait()

    def inside_rows(first, sublane):
        at = first + sublane
        above = jnp.where(at < OFF, has_up, one)
        return jnp.where(at >= OFF + nrow, has_down, above)

    def unpack_body(t, carry):
        src = pl.ds(pl.multiple_of(8 * t, 8), 8)
        dst = pl.ds(pl.multiple_of(OFF - HALO + 8 * t, 8), 8)
        rowmask = inside_rows(OFF - HALO + 8 * t, sub)
        from_left = crecv[0, src, :] * (rowmask * has_left)
        from_right = crecv[1, src, :] * (rowmask * has_right)
        for k in range(12):
            low = pltpu.roll(from_left, (LANES - HALO - HALO * k) % LANES, axis=1)
            high = pltpu.roll(from_right, (-HALO * k) % LANES, axis=1) if k else from_right
            tile = jnp.where(lane < HALO, high, jnp.where(lane >= LANES - HALO, low, 0.0))
            if k < 8:
                rbuf[nu, k, dst, :] = tile
            else:
                cbuf[k - 8, nu, dst, :] = tile
        return carry
    lax.fori_loop(0, (nrow + 2 * HALO) // 8, unpack_body, 0)

    def sunpack_body(t, carry):
        src = pl.ds(pl.multiple_of(16 * t, 16), 16)
        rowmask = inside_rows(16 * t, lax.broadcasted_iota(jnp.int32, (16, LANES), 0))
        for part in range(2):
            cols = slice(part * LANES, (part + 1) * LANES)
            from_left = srecv[0, src, cols].astype(jnp.float32) * (rowmask * has_left)
            from_right = srecv[1, src, cols].astype(jnp.float32) * (rowmask * has_right)
            for k in range(16 if part == 0 else 9):
                low = pltpu.roll(from_left, (LANES - HALO - HALO * k) % LANES, axis=1)
                high = pltpu.roll(from_right, (-HALO * k) % LANES, axis=1) if k else from_right
                sfull[nu, 16 * part + k, src, :] = jnp.where(
                    lane16 < HALO, high, jnp.where(lane16 >= LANES - HALO, low, 0.0))
        return carry
    lax.fori_loop(0, (nrow + 2 * OFF) // 16, sunpack_body, 0)

    colmask = [jnp.ones((8, LANES), jnp.float32)] * nu + [
        jnp.where(lane < LANES // 2, has_right, has_left)]

    def sym_body(t, carry):
        at = OFF - HALO + 8 * t
        here = pl.ds(pl.multiple_of(at, 8), 8)
        rowmask = inside_rows(at, sub) * 0.5
        masks = {b: ring_shifts([m * rowmask for m in colmask], -b, lane) for b in range(-2, 3)}
        for o, (a, b) in enumerate(OFFSETS):
            own = ring_shifts([sfull[u, o, here, :] for u in range(nt)], -b, lane)
            for u in range(nt):
                mirror = sfull[u, 24 - o, pl.ds(at + a, 8), :]
                symp[u, o, here, :] = (own[u] + mirror) * masks[b][u]
        return carry
    lax.fori_loop(0, (nrow + 2 * HALO) // 8, sym_body, 0)

    def lap_body(t, carry):
        at = OFF - HALO + 8 * t
        here = pl.ds(pl.multiple_of(at, 8), 8)
        above, below = pl.ds(at - 1, 8), pl.ds(at + 1, 8)
        tiles = lambda k, rows: [cbuf[k, u, rows, :] for u in range(nt)]
        kap, con, inv, msk = (tiles(k, here) for k in range(4))
        con_n = ring_shifts(con, 1, lane)
        east = [0.5 * (con[u] + con_n[u]) for u in range(nt)]
        west = ring_shifts(east, -1, lane)
        inv_e, inv_w = ring_shifts(inv, 1, lane), ring_shifts(inv, -1, lane)
        msk_e, msk_w = ring_shifts(msk, 1, lane), ring_shifts(msk, -1, lane)
        for u in range(nt):
            north = 0.5 * (con[u] + cbuf[1, u, above, :])
            south = 0.5 * (con[u] + cbuf[1, u, below, :])
            diag = kap[u] + north + south + west[u] + east[u]
            lap[0, u, here, :] = inv[u] * diag * msk[u]
            lap[1, u, here, :] = inv[u] * north * cbuf[3, u, above, :]
            lap[2, u, here, :] = inv[u] * south * cbuf[3, u, below, :]
            lap[3, u, here, :] = inv_w[u] * west[u] * msk[u]
            lap[4, u, here, :] = inv_e[u] * east[u] * msk[u]
            lap[5, u, here, :] = msk[u] * diag
            lap[6, u, here, :] = msk[u] * north
            lap[7, u, here, :] = msk[u] * south
            lap[8, u, here, :] = msk_w[u] * west[u]
            lap[9, u, here, :] = msk_e[u] * east[u]
            lap[10, u, here, :] = 1.0 - msk[u]
        return carry
    lax.fori_loop(0, (nrow + 2 * HALO) // 8, lap_body, 0)

    def apply_m(src, dst, start, count):
        def body(t, carry):
            at = start + 8 * t
            for p0 in range(0, PROBES, 2):
                pair_p = (p0, p0 + 1)
                field = {(p, a, u): src[u, p, pl.ds(at + a, 8), :] for p in pair_p for a in range(-2, 3) for u in range(nt)}
                total = {}
                for b in range(-2, 3):
                    part = {}
                    for a in range(-2, 3):
                        o = (a + 2) * 5 + b + 2
                        for u in range(nt):
                            weight = symp[u, o, pl.ds(at, 8), :]
                            for p in pair_p:
                                term = weight * field[p, a, u]
                                part[p, u] = term if a == -2 else part[p, u] + term
                    for p in pair_p:
                        moved = ring_shifts([part[p, u] for u in range(nt)], b, lane)
                        for u in range(nt):
                            total[p, u] = moved[u] if b == -2 else total[p, u] + moved[u]
                for p in pair_p:
                    for u in range(nt):
                        dst[u, p, pl.ds(at, 8), :] = total[p, u]
            return carry
        lax.fori_loop(0, count, body, 0)

    def half_laplace(first, src, at, p, coefs):
        centre = [src[u, p, pl.ds(at, 8), :] for u in range(nt)]
        to_east = ring_shifts([coefs[3][u] * centre[u] for u in range(nt)], 1, lane)
        to_west = ring_shifts([coefs[4][u] * centre[u] for u in range(nt)], -1, lane)
        out = []
        for u in range(nt):
            across = to_east[u] + to_west[u]
            along = coefs[1][u] * src[u, p, pl.ds(at - 1, 8), :] + coefs[2][u] * src[u, p, pl.ds(at + 1, 8), :]
            out.append(coefs[0][u] * centre[u] - (across + along))
        return out

    def apply_a(src, dst, start_in, count_in, start, count, keep):
        def inner(t, carry):
            at = start_in + 8 * t
            coefs = [[lap[k, u, pl.ds(at, 8), :] for u in range(nt)] for k in range(5)]
            for p in range(PROBES):
                out = half_laplace(0, src, at, p, coefs)
                for u in range(nt):
                    tbuf[u, p, pl.ds(at, 8), :] = out[u]
            return carry
        lax.fori_loop(0, count_in, inner, 0)

        def outer(t, carry):
            at = start + 8 * t
            coefs = [[lap[5 + k, u, pl.ds(at, 8), :] for u in range(nt)] for k in range(6)]
            for p in range(PROBES):
                out = half_laplace(5, tbuf, at, p, coefs)
                for u in range(keep):
                    dst[u, p, pl.ds(at, 8), :] = out[u] + coefs[5][u] * src[u, p, pl.ds(at, 8), :]
            return carry
        lax.fori_loop(0, count, outer, 0)

    pairs = [(k, l) for k in range(8) for l in range(k, 8)]

    def gram(first, second):
        def body(i, acc):
            u = i // (nrow // 8)
            rows = pl.ds(pl.multiple_of(OFF + 8 * (i % (nrow // 8)), 8), 8)
            a = [first[u, p, rows, :] for p in range(PROBES)]
            b = [second[u, p, rows, :] for p in range(PROBES)]
            return tuple(acc[n] + a[k] * b[l] for n, (k, l) in enumerate(pairs))
        start = tuple(jnp.zeros((8, LANES), jnp.float32) for _ in pairs)
        acc = lax.fori_loop(0, nu * (nrow // 8), body, start)
        return [jnp.sum(a, axis=0, keepdims=True) for a in acc]

    def gather(total, m, sums):
        index = {}
        for n, (k, l) in enumerate(pairs):
            index[k, l] = index[l, k] = sums[n]
        for l in range(8):
            stacked = jnp.broadcast_to(index[0, l], (8, LANES))
            for k in range(1, 8):
                stacked = jnp.where(sub == k, index[k, l], stacked)
            total = jnp.where(lane == 8 * m + l, jnp.sum(stacked, axis=1, keepdims=True), total)
        return total

    last = nrow + OFF
    partial = jnp.zeros((8, LANES), jnp.float32)
    apply_m(rbuf, zbuf, OFF - 8, (nrow + 16) // 8)
    partial = gather(partial, 0, gram(rbuf, zbuf))
    apply_a(zbuf, wbuf, OFF - 8, (nrow + 16) // 8, OFF - 4, (nrow + 8) // 8, nt)
    partial = gather(partial, 1, gram(zbuf, wbuf))
    apply_m(wbuf, ybuf, OFF - 2, (nrow + 8) // 8)
    partial = gather(partial, 2, gram(wbuf, ybuf))
    vbuf = sfull
    apply_a(ybuf, vbuf, OFF - 1, (nrow + 8) // 8, OFF, nrow // 8, nu)
    partial = gather(partial, 3, gram(ybuf, vbuf))

    def exchange(value, buf, mine, partners, ssems, rsems, count):
        buf[mine] = value
        copies = []
        for d, who in enumerate(partners):
            copies.append(pltpu.make_async_remote_copy(
                src_ref=buf.at[mine], dst_ref=buf.at[mine], send_sem=ssems.at[d], recv_sem=rsems.at[mine],
                device_id=who, device_id_type=MESH))
        for copy in copies:
            copy.start()
        for d in range(1, count):
            slot = (mine + d) % count
            pltpu.make_async_copy(buf.at[slot], buf.at[slot], rsems.at[slot]).wait()
        for copy in copies:
            copy.wait_send()
        total = buf[0]
        for k in range(1, count):
            total = total + buf[k]
        return total

    g = exchange(partial, grams1, mine1, partners1, s1, r1, group1)
    g = exchange(g, grams2, pair, partners2, s2, r2, group2)

    g1s, g2s, g3s, g4s = (splats(g, 8 * m) for m in range(4))
    shifted = lambda m: pltpu.roll(g, (-8 * m) % LANES, axis=1) if m else g
    g1r, g2r = rows_of(shifted(0)), rows_of(shifted(1))
    fact2, fact1 = factor(g2s), factor(g1s)
    add = lambda x, y: [a + b for a, b in zip(x, y)]
    minus = lambda x, y: [a - b for a, b in zip(x, y)]
    alpha = substitute(fact2, g1r)
    alpha_s = splats(stack_rows(alpha, sub), 0)
    g3_alpha = product(g3s, alpha)
    gamma = minus(minus(g1r, product(g2s, alpha)), product_t(alpha_s, minus(g2r, g3_alpha)))
    beta = substitute(fact1, gamma)
    eye = [jnp.where(lane == k, 1.0, 0.0) for k in range(8)]
    b_rows = add(beta, eye)
    b_s = splats(stack_rows(b_rows, sub), 0)
    curv = minus(
        product_t(b_s, minus(product(g2s, b_rows), g3_alpha)),
        product_t(alpha_s, minus(product(g3s, b_rows), product(g4s, alpha))))
    curv_s = splats(stack_rows(curv, sub), 0)
    curv_s = [[0.5 * (curv_s[k][l] + curv_s[l][k]) for l in range(8)] for k in range(8)]
    alpha1 = substitute(factor(curv_s), gamma)
    c1 = add(alpha, product(b_s, alpha1))
    c2 = product(alpha_s, alpha1)
    for m, rows in enumerate((c1, c2)):
        spread = splats(stack_rows(rows, sub), 0)
        for k in range(8):
            for l in range(8):
                coef[m, l, k] = spread[k][l]

    outs = []
    for l in range(PROBES):
        outs.append(pltpu.make_async_copy(xs.at[l], x_out.at[l], osem.at[l]))
        outs.append(pltpu.make_async_copy(rs.at[l], r_out.at[l], osem.at[8 + l]))
    for l0 in range(0, PROBES, 2):
        ca = [[coef[0, l, k] for k in range(8)] for l in (l0, l0 + 1)]
        cb = [[coef[1, l, k] for k in range(8)] for l in (l0, l0 + 1)]

        def mix_body(t, carry, l0=l0, ca=ca, cb=cb):
            rows = pl.ds(pl.multiple_of(OFF + 8 * t, 8), 8)
            out = pl.ds(pl.multiple_of(8 * t, 8), 8)
            for u in range(nu):
                cols = slice(u * LANES, (u + 1) * LANES)
                for first, second, dst, base, sign in ((zbuf, ybuf, xs, None, 1.0), (wbuf, vbuf, rs, rbuf, -1.0)):
                    f = [first[u, k, rows, :] for k in range(8)]
                    s = [second[u, k, rows, :] for k in range(8)]
                    for i in range(2):
                        total = ca[i][0] * f[0]
                        for k in range(1, 8):
                            total = total + ca[i][k] * f[k]
                        for k in range(8):
                            total = total - cb[i][k] * s[k]
                        if base is not None:
                            total = base[u, l0 + i, rows, :] - total
                        dst[l0 + i, out, cols] = total
            return carry
        lax.fori_loop(0, nrow // 8, mix_body, 0)
        for copy in outs[2 * l0 : 2 * l0 + 4]:
            copy.start()
    for copy in outs:
        copy.wait()


def shards(probes, kappa_sq, conduct, inv_mass, spai, sea_mask):
    _, nrow, ncol = probes.shape
    rows_n, cols_n = lax.axis_size("row"), lax.axis_size("col")
    nu = ncol // LANES
    nt = nu + 1
    ext = nrow + 2 * OFF
    f32, bf16 = jnp.float32, jnp.bfloat16
    field = pltpu.VMEM((nt, PROBES, ext, LANES), f32)
    dma = pltpu.SemaphoreType.DMA
    scratch = [
        field, field, field, field, field,
        pltpu.VMEM((25, ext, ncol), bf16),
        pltpu.VMEM((nt, 25, ext, LANES), f32),
        pltpu.VMEM((nt, 25, ext, LANES), f32),
        pltpu.VMEM((4, nt, ext, LANES), f32),
        pltpu.VMEM((11, nt, ext, LANES), f32),
        pltpu.VMEM((2, PROBES, HALO, ncol), f32),
        pltpu.VMEM((2, 3, HALO, ncol), f32),
        pltpu.VMEM((2, HALO, ncol), jnp.int32),
        pltpu.VMEM((nrow, ncol), jnp.int32),
        pltpu.VMEM((2, nrow, LANES), f32),
        pltpu.VMEM((2, nrow, 2 * LANES), bf16),
        pltpu.VMEM((2, nrow + 2 * HALO, LANES), f32),
        pltpu.VMEM((2, ext, 2 * LANES), bf16),
        pltpu.VMEM((2 * cols_n, 8, LANES), f32),
        pltpu.VMEM((rows_n // 2, 8, LANES), f32),
        pltpu.VMEM((2, 8, 8, 8, LANES), f32),
        pltpu.VMEM((PROBES, nrow, ncol), f32),
        pltpu.VMEM((PROBES, nrow, ncol), f32),
        dma((2 + 4 * nu,)),
        dma((24,)), dma((24,)),
        dma((2 * cols_n,)), dma((2 * cols_n,)),
        dma((rows_n // 2,)), dma((rows_n // 2,)),
        dma((16,)),
    ]
    out = jax.ShapeDtypeStruct(probes.shape, f32)
    return pl.pallas_call(
        functools.partial(kernel, nrow, ncol, rows_n, cols_n),
        out_shape=(out, out),
        in_specs=[pl.BlockSpec(memory_space=pl.ANY)] * 6,
        out_specs=(pl.BlockSpec(memory_space=pl.ANY),) * 2,
        scratch_shapes=scratch,
        compiler_params=pltpu.CompilerParams(
            collective_id=0, has_side_effects=True, vmem_limit_bytes=48 * 1024 * 1024),
    )(probes, kappa_sq, conduct, inv_mass, spai, sea_mask)


def solution(mesh):
    field = P(None, "row", "col")
    cell = P("row", "col")
    return jax.shard_map(
        shards, mesh=mesh, in_specs=(field, cell, cell, cell, field, cell),
        out_specs=(field, field), check_vma=False)
```

```python
import functools

import jax
import jax.numpy as jnp
from jax import lax
from jax.experimental import pallas as pl
from jax.experimental.pallas import tpu as pltpu
from jax.sharding import PartitionSpec as P

MESH = pl.DeviceIdType.MESH
PROBES = 8
LANES = 128
HALO = 8
OFF = 16
OFFSETS = [(o // 5 - 2, o % 5 - 2) for o in range(25)]


def tile_shift(tiles, place, step, lane):
    if step == 0:
        return tiles[place]
    count = len(tiles)
    here = pltpu.roll(tiles[place], (-step) % LANES, axis=1)
    if step > 0:
        there = pltpu.roll(tiles[(place + 1) % count], (-step) % LANES, axis=1)
        return jnp.where(lane < LANES - step, here, there)
    there = pltpu.roll(tiles[(place - 1) % count], (-step) % LANES, axis=1)
    return jnp.where(lane >= -step, here, there)


def ring_shifts(tiles, step, lane):
    if step == 0:
        return list(tiles)
    count = len(tiles)
    rolled = [pltpu.roll(tile, (-step) % LANES, axis=1) for tile in tiles]
    if step > 0:
        return [jnp.where(lane < LANES - step, rolled[u], rolled[(u + 1) % count]) for u in range(count)]
    return [jnp.where(lane >= -step, rolled[u], rolled[(u - 1) % count]) for u in range(count)]


def splats(matrix, first):
    out = [[None] * 8 for _ in range(8)]
    for col in range(8):
        wide = jnp.broadcast_to(matrix[:, first + col : first + col + 1], (8, LANES))
        for row in range(8):
            out[row][col] = jnp.broadcast_to(wide[row : row + 1, :], (8, LANES))
    return out


def rows_of(matrix):
    return [jnp.broadcast_to(matrix[k : k + 1, :], (8, LANES)) for k in range(8)]


def stack_rows(rows, sub):
    out = rows[0]
    for k in range(1, 8):
        out = jnp.where(sub == k, rows[k], out)
    return out


def product(left, rows):
    out = []
    for i in range(8):
        total = left[i][0] * rows[0]
        for j in range(1, 8):
            total = total + left[i][j] * rows[j]
        out.append(total)
    return out


def product_t(left, rows):
    return product([[left[j][i] for j in range(8)] for i in range(8)], rows)


def factor(entries):
    a = [list(r) for r in entries]
    mult = [[None] * 8 for _ in range(8)]
    inverse = []
    for j in range(8):
        inv = 1.0 / a[j][j]
        inverse.append(inv)
        for k in range(j + 1, 8):
            mult[k][j] = a[j][k] * inv
            for m in range(k, 8):
                a[k][m] = a[k][m] - mult[k][j] * a[j][m]
    return mult, inverse


def substitute(fact, rows):
    mult, inverse = fact
    y = list(rows)
    for j in range(8):
        for k in range(j + 1, 8):
            y[k] = y[k] - mult[k][j] * y[j]
    y = [y[j] * inverse[j] for j in range(8)]
    for j in range(7, -1, -1):
        for k in range(j):
            y[k] = y[k] - mult[j][k] * y[j]
    return y


def kernel(
    nrow, ncol, rows_n, cols_n,
    probes, kappa, conduct, inv_mass, spai, sea,
    x_out, r_out,
    rbuf, zbuf, wbuf, ybuf, tbuf, sraw, sfull, symp, cbuf, lap,
    fedge, sedge, fland, sland, seaown, cpack, spack, crecv, srecv,
    grams, coef, xs, rs, ps, ws, vbuf,
    lsem, ssem, rsem, gsend, grecv, osem,
):
    nu = ncol // LANES
    nt = nu + 1
    row = lax.axis_index("row")
    col = lax.axis_index("col")
    core = row % 2
    pair = row // 2
    group1 = 2 * cols_n
    group2 = rows_n // 2
    up, down = (row + rows_n - 1) % rows_n, (row + 1) % rows_n
    left, right = (col + cols_n - 1) % cols_n, (col + 1) % cols_n
    mine1 = core * cols_n + col

    partners1 = []
    for d in range(1, group1):
        q = (mine1 + d) % group1
        partners1.append((row - core + q // cols_n, q % cols_n))
    partners2 = []
    for d in range(1, group2):
        q = (pair + d) % group2
        partners2.append((2 * q + core, col))
    around = [(up, left), (up, col), (up, right), (row, left), (row, right), (down, left), (down, col), (down, right)]

    barrier = pltpu.get_barrier_semaphore()
    for who in around + partners1 + partners2:
        pl.semaphore_signal(barrier, inc=1, device_id=who, device_id_type=MESH)

    local = []
    local.append(pltpu.make_async_copy(spai, sraw, lsem.at[0]))
    for u in range(nu):
        local.append(pltpu.make_async_copy(
            probes.at[:, :, pl.ds(u * LANES, LANES)], rbuf.at[u, :, pl.ds(OFF, nrow), :], lsem.at[1 + u]))
    for k, field in enumerate((kappa, conduct, inv_mass)):
        for u in range(nu):
            local.append(pltpu.make_async_copy(
                field.at[:, pl.ds(u * LANES, LANES)], cbuf.at[k, u, pl.ds(OFF, nrow), :], lsem.at[1 + nu + k * nu + u]))
    local.append(pltpu.make_async_copy(sea, seaown, lsem.at[1 + 4 * nu]))
    for copy in local:
        copy.start()

    lane = lax.broadcasted_iota(jnp.int32, (8, LANES), 1)
    sub = lax.broadcasted_iota(jnp.int32, (8, LANES), 0)
    lane16 = lax.broadcasted_iota(jnp.int32, (16, LANES), 1)
    edge_lanes = jnp.logical_or(lane < HALO, lane >= LANES - HALO)
    edge_lanes16 = jnp.logical_or(lane16 < HALO, lane16 >= LANES - HALO)

    for copy in local[1:]:
        copy.wait()

    def sea_body(t, carry):
        for u in range(nu):
            rows = pl.ds(pl.multiple_of(8 * t, 8), 8)
            dst = pl.ds(pl.multiple_of(OFF + 8 * t, 8), 8)
            cbuf[3, u, dst, :] = seaown[rows, u * LANES : (u + 1) * LANES].astype(jnp.float32)
        return carry
    lax.fori_loop(0, nrow // 8, sea_body, 0)

    for side, at in ((0, OFF + nrow - HALO), (1, OFF)):
        for u in range(nu):
            cols = slice(u * LANES, (u + 1) * LANES)
            for k in range(12):
                fedge[side, k, :, cols] = rbuf[u, k, at : at + 8, :] if k < 8 else cbuf[k - 8, u, at : at + 8, :]

    def pack_body(t, carry):
        src = pl.ds(pl.multiple_of(OFF + 8 * t, 8), 8)
        dst = pl.ds(pl.multiple_of(8 * t, 8), 8)
        group = lane // HALO
        for side, u in ((0, 0), (1, nu - 1)):
            total = jnp.zeros((8, LANES), jnp.float32)
            for k in range(12):
                item = rbuf[u, k, src, :] if k < 8 else cbuf[k - 8, u, src, :]
                moved = pltpu.roll(item, HALO * k, axis=1) if k else item
                total = jnp.where(group == (k - side) % 16, moved, total)
            cpack[side, dst, :] = total
        return carry
    lax.fori_loop(0, nrow // 8, pack_body, 0)

    local[0].wait()

    def spack_body(t, carry):
        src = pl.ds(pl.multiple_of(16 * t, 16), 16)
        full = pl.ds(pl.multiple_of(OFF + 16 * t, 16), 16)
        group = lane16 // HALO
        for o in range(25):
            tiles = []
            for u in range(nu):
                tile = sraw[o, src, u * LANES : (u + 1) * LANES].astype(jnp.float32)
                sfull[u, o, full, :] = tile
                tiles.append(tile)
            if o % 16 == 0:
                totals = [jnp.zeros((16, LANES), jnp.float32)] * 2
            for side, u in ((0, 0), (1, nu - 1)):
                shift = (HALO * o) % LANES
                moved = pltpu.roll(tiles[u], shift, axis=1) if shift else tiles[u]
                totals[side] = jnp.where(group == (o - side) % 16, moved, totals[side])
            if o % 16 == 15 or o == 24:
                part = o // 16
                for side in range(2):
                    spack[side, src, part * LANES : (part + 1) * LANES] = totals[side].astype(jnp.bfloat16)
        return carry
    lax.fori_loop(0, nrow // 16, spack_body, 0)

    for side, at in ((0, OFF + nrow - HALO), (1, OFF)):
        for u in range(nu):
            cols = slice(u * LANES, (u + 1) * LANES)
            for j in range(13):
                first = sfull[u, 2 * j, at : at + 8, :]
                second = sfull[u, min(2 * j + 1, 24), at : at + 8, :]
                sedge[side, j, :, cols] = jnp.concatenate([first, second], axis=0).astype(jnp.bfloat16)

    pl.semaphore_wait(barrier, len(around) + len(partners1) + len(partners2))

    def remote(index, src, dst, who):
        return pltpu.make_async_remote_copy(
            src_ref=src, dst_ref=dst, send_sem=ssem.at[index], recv_sem=rsem.at[index],
            device_id=who, device_id_type=MESH)

    row_copies = []
    for side, who in ((0, down), (1, up)):
        row_copies.append(remote(2 * side, sedge.at[side], sland.at[side], (who, col)))
        row_copies.append(remote(2 * side + 1, fedge.at[side], fland.at[side], (who, col)))
    col_copies = []
    for side, who in ((0, left), (1, right)):
        to = 1 - side
        base = 4 + 6 * side
        col_copies += [
            remote(base, spack.at[side, pl.ds(0, OFF), :], srecv.at[to, pl.ds(OFF + nrow, OFF), :], (up, who)),
            remote(base + 1, cpack.at[side, pl.ds(0, HALO), :], crecv.at[to, pl.ds(HALO + nrow, HALO), :], (up, who)),
            remote(base + 2, spack.at[side, pl.ds(nrow - OFF, OFF), :], srecv.at[to, pl.ds(0, OFF), :], (down, who)),
            remote(base + 3, cpack.at[side, pl.ds(nrow - HALO, HALO), :], crecv.at[to, pl.ds(0, HALO), :], (down, who)),
            remote(base + 4, spack.at[side], srecv.at[to, pl.ds(OFF, nrow), :], (row, who)),
            remote(base + 5, cpack.at[side], crecv.at[to, pl.ds(HALO, nrow), :], (row, who)),
        ]
    for copy in col_copies + row_copies:
        copy.start()

    one = jnp.float32(1.0)
    zero = jnp.float32(0.0)
    has_up = jnp.where(row > 0, one, zero)
    has_down = jnp.where(row < rows_n - 1, one, zero)
    has_left = jnp.where(col > 0, one, zero)
    has_right = jnp.where(col < cols_n - 1, one, zero)

    def rotate_body(t, carry):
        here = pl.ds(pl.multiple_of(OFF + 8 * t, 8), 8)
        for o, (a, b) in enumerate(OFFSETS):
            if b:
                for u in range(nu):
                    symp[u, o, here, :] = pltpu.roll(sfull[u, o, here, :], b % LANES, axis=1)
        return carry
    lax.fori_loop(0, nrow // 8, rotate_body, 0)

    for copy in row_copies:
        copy.wait_recv()
    for side, keep, at in ((0, has_up, OFF - HALO), (1, has_down, OFF + nrow)):
        for u in range(nu):
            cols = slice(u * LANES, (u + 1) * LANES)
            for k in range(12):
                item = fland[side, k, :, cols] * keep
                if k < 8:
                    rbuf[u, k, at : at + 8, :] = item
                else:
                    cbuf[k - 8, u, at : at + 8, :] = item
            for j in range(13):
                both = sland[side, j, :, cols].astype(jnp.float32) * keep
                sfull[u, 2 * j, at : at + 8, :] = both[0:8]
                if j < 12:
                    sfull[u, 2 * j + 1, at : at + 8, :] = both[8:16]

    for copy in col_copies:
        copy.wait_recv()

    def inside_rows(first, sublane):
        at = first + sublane
        above = jnp.where(at < OFF, has_up, one)
        return jnp.where(at >= OFF + nrow, has_down, above)

    def unpack_body(t, carry):
        src = pl.ds(pl.multiple_of(8 * t, 8), 8)
        dst = pl.ds(pl.multiple_of(OFF - HALO + 8 * t, 8), 8)
        rowmask = inside_rows(OFF - HALO + 8 * t, sub)
        from_left = crecv[0, src, :] * (rowmask * has_left)
        from_right = crecv[1, src, :] * (rowmask * has_right)
        odd = (lane // HALO) % 2 == 1
        merged = (jnp.where(odd, from_left, from_right), jnp.where(odd, from_right, from_left))
        for k in range(12):
            moved = pltpu.roll(merged[k % 2], (-HALO * k) % LANES, axis=1) if k else merged[0]
            tile = jnp.where(edge_lanes, moved, 0.0)
            if k < 8:
                rbuf[nu, k, dst, :] = tile
            else:
                cbuf[k - 8, nu, dst, :] = tile
        return carry
    lax.fori_loop(0, (nrow + 2 * HALO) // 8, unpack_body, 0)

    def sunpack_body(t, carry):
        src = pl.ds(pl.multiple_of(16 * t, 16), 16)
        rowmask = inside_rows(16 * t, lax.broadcasted_iota(jnp.int32, (16, LANES), 0))
        for part in range(2):
            cols = slice(part * LANES, (part + 1) * LANES)
            from_left = srecv[0, src, cols].astype(jnp.float32) * (rowmask * has_left)
            from_right = srecv[1, src, cols].astype(jnp.float32) * (rowmask * has_right)
            odd = (lane16 // HALO) % 2 == 1
            merged = (jnp.where(odd, from_left, from_right), jnp.where(odd, from_right, from_left))
            for k in range(16 if part == 0 else 9):
                moved = pltpu.roll(merged[k % 2], (-HALO * k) % LANES, axis=1) if k else merged[0]
                sfull[nu, 16 * part + k, src, :] = jnp.where(edge_lanes16, moved, 0.0)
        return carry
    lax.fori_loop(0, (nrow + 2 * OFF) // 16, sunpack_body, 0)

    colmask = [jnp.ones((8, LANES), jnp.float32)] * nu + [
        jnp.where(lane < LANES // 2, has_right, has_left)]

    def sym_tile(at, rotated):
        here = pl.ds(at, 8)
        rowmask = inside_rows(at, sub) * 0.5
        masks = {b: ring_shifts([m * rowmask for m in colmask], -b, lane) for b in range(-2, 3)}
        for o, (a, b) in enumerate(OFFSETS):
            if b == 0:
                own = [sfull[u, o, here, :] for u in range(nt)]
            else:
                rolled = [
                    symp[u, o, here, :] if rotated and u < nu else pltpu.roll(sfull[u, o, here, :], b % LANES, axis=1)
                    for u in range(nt)]
                if b < 0:
                    own = [jnp.where(lane < LANES + b, rolled[u], rolled[(u + 1) % nt]) for u in range(nt)]
                else:
                    own = [jnp.where(lane >= b, rolled[u], rolled[(u - 1) % nt]) for u in range(nt)]
            for u in range(nt):
                mirror = sfull[u, 24 - o, pl.ds(at + a, 8), :]
                symp[u, o, here, :] = (own[u] + mirror) * masks[b][u]

    def sym_body(t, carry):
        sym_tile(pl.multiple_of(OFF + 8 * t, 8), True)
        return carry
    lax.fori_loop(0, nrow // 8, sym_body, 0)

    def sym_halo_body(t, carry):
        sym_tile(pl.multiple_of(OFF - HALO + t * (nrow + HALO), 8), False)
        return carry
    lax.fori_loop(0, 2, sym_halo_body, 0)

    def lap_body(t, carry):
        at = OFF - HALO + 8 * t
        here = pl.ds(pl.multiple_of(at, 8), 8)
        above, below = pl.ds(at - 1, 8), pl.ds(at + 1, 8)
        tiles = lambda k, rows: [cbuf[k, u, rows, :] for u in range(nt)]
        kap, con, inv, msk = (tiles(k, here) for k in range(4))
        con_n = ring_shifts(con, 1, lane)
        east = [0.5 * (con[u] + con_n[u]) for u in range(nt)]
        west = ring_shifts(east, -1, lane)
        inv_e, inv_w = ring_shifts(inv, 1, lane), ring_shifts(inv, -1, lane)
        msk_e, msk_w = ring_shifts(msk, 1, lane), ring_shifts(msk, -1, lane)
        for u in range(nt):
            north = 0.5 * (con[u] + cbuf[1, u, above, :])
            south = 0.5 * (con[u] + cbuf[1, u, below, :])
            diag = kap[u] + north + south + west[u] + east[u]
            lap[0, u, here, :] = inv[u] * diag * msk[u]
            lap[1, u, here, :] = inv[u] * north * cbuf[3, u, above, :]
            lap[2, u, here, :] = inv[u] * south * cbuf[3, u, below, :]
            lap[3, u, here, :] = inv_w[u] * west[u] * msk[u]
            lap[4, u, here, :] = inv_e[u] * east[u] * msk[u]
            lap[5, u, here, :] = msk[u] * diag
            lap[6, u, here, :] = msk[u] * north
            lap[7, u, here, :] = msk[u] * south
            lap[8, u, here, :] = msk_w[u] * west[u]
            lap[9, u, here, :] = msk_e[u] * east[u]
            lap[10, u, here, :] = 1.0 - msk[u]
            if u < nu:
                lap[11, u, here, :] = 1.0 / inv[u]
        return carry
    lax.fori_loop(0, (nrow + 2 * HALO) // 8, lap_body, 0)

    def apply_m(src, dst, start, count):
        def body(t, carry):
            at = start + 8 * t
            for p0 in range(0, PROBES, 2):
                pair_p = (p0, p0 + 1)
                field = {(p, a, u): src[u, p, pl.ds(at + a, 8), :] for p in pair_p for a in range(-2, 3) for u in range(nt)}
                total = {}
                for b in range(-2, 3):
                    part = {}
                    for a in range(-2, 3):
                        o = (a + 2) * 5 + b + 2
                        for u in range(nt):
                            weight = symp[u, o, pl.ds(at, 8), :]
                            for p in pair_p:
                                term = weight * field[p, a, u]
                                part[p, u] = term if a == -2 else part[p, u] + term
                    for p in pair_p:
                        moved = ring_shifts([part[p, u] for u in range(nt)], b, lane)
                        for u in range(nt):
                            total[p, u] = moved[u] if b == -2 else total[p, u] + moved[u]
                for p in pair_p:
                    for u in range(nt):
                        dst[u, p, pl.ds(at, 8), :] = total[p, u]
            return carry
        lax.fori_loop(0, count, body, 0)

    def half_laplace(first, src, at, p, coefs):
        centre = [src[u, p, pl.ds(at, 8), :] for u in range(nt)]
        to_east = ring_shifts([coefs[3][u] * centre[u] for u in range(nt)], 1, lane)
        to_west = ring_shifts([coefs[4][u] * centre[u] for u in range(nt)], -1, lane)
        out = []
        for u in range(nt):
            across = to_east[u] + to_west[u]
            along = coefs[1][u] * src[u, p, pl.ds(at - 1, 8), :] + coefs[2][u] * src[u, p, pl.ds(at + 1, 8), :]
            out.append(coefs[0][u] * centre[u] - (across + along))
        return out

    def inner_a(src, start, count):
        def body(t, carry):
            at = start + 8 * t
            coefs = [[lap[k, u, pl.ds(at, 8), :] for u in range(nt)] for k in range(5)]
            for p in range(PROBES):
                out = half_laplace(0, src, at, p, coefs)
                for u in range(nt):
                    tbuf[u, p, pl.ds(at, 8), :] = out[u]
            return carry
        lax.fori_loop(0, count, body, 0)

    def outer_a(src, dst, start, count, keep):
        def body(t, carry):
            at = start + 8 * t
            coefs = [[lap[5 + k, u, pl.ds(at, 8), :] for u in range(nt)] for k in range(6)]
            for p in range(PROBES):
                out = half_laplace(5, tbuf, at, p, coefs)
                for u in range(keep):
                    dst[u, p, pl.ds(at, 8), :] = out[u] + coefs[5][u] * src[u, p, pl.ds(at, 8), :]
            return carry
        lax.fori_loop(0, count, body, 0)

    pairs = [(k, l) for k in range(8) for l in range(k, 8)]

    groups = -(-len(pairs) // 8)

    def gram(terms):
        def body(i, acc):
            u = i // (nrow // 8)
            rows = pl.ds(pl.multiple_of(OFF + 8 * (i % (nrow // 8)), 8), 8)
            for first, second, weight in terms:
                a = [first[u, p, rows, :] for p in range(PROBES)]
                if weight is not None:
                    w = lap[weight, u, rows, :]
                    a = [w * x for x in a]
                b = [second[u, p, rows, :] for p in range(PROBES)]
                acc = tuple(acc[n] + a[k] * b[l] for n, (k, l) in enumerate(pairs))
            return acc
        start = tuple(jnp.zeros((8, LANES), jnp.float32) for _ in pairs)
        return lax.fori_loop(0, nu * (nrow // 8), body, start)

    def to_lanes(total, first, acc):
        for j in range(groups):
            stacked = None
            for s in range(8):
                if 8 * j + s < len(acc):
                    entry = jnp.broadcast_to(jnp.sum(acc[8 * j + s], axis=0, keepdims=True), (8, LANES))
                    stacked = entry if stacked is None else jnp.where(sub == s, entry, stacked)
            total = jnp.where(lane == first + j, jnp.sum(stacked, axis=1, keepdims=True), total)
        return total

    def one_row(total):
        spread = pltpu.roll(total, 0, axis=1, stride=16, stride_axis=0)
        return jnp.sum(spread, axis=0, keepdims=True)

    def entries(line, first):
        out = [[None] * 8 for _ in range(8)]
        for n, (k, l) in enumerate(pairs):
            at = 16 * (n % 8) + first + n // 8
            out[k][l] = out[l][k] = jnp.broadcast_to(line[:, at : at + 1], (8, LANES))
        return out

    def entry_rows(spread):
        out = []
        for k in range(8):
            line = spread[k][0]
            for l in range(1, 8):
                line = jnp.where(lane == l, spread[k][l], line)
            out.append(line)
        return out

    def post(step, phase, value):
        mine, partners, count = ((mine1, partners1, group1), (pair, partners2, group2))[phase]
        buf = grams.at[step, phase]
        buf[mine] = value
        copies = [pltpu.make_async_remote_copy(
            src_ref=buf.at[mine], dst_ref=buf.at[mine],
            send_sem=gsend.at[step, phase, d], recv_sem=grecv.at[step, phase, mine],
            device_id=who, device_id_type=MESH) for d, who in enumerate(partners)]
        for copy in copies:
            copy.start()

        def finish():
            for d in range(1, count):
                slot = (mine + d) % count
                pltpu.make_async_copy(buf.at[slot], buf.at[slot], grecv.at[step, phase, slot]).wait()
            terms = [buf[k] for k in range(count)]
            while len(terms) > 1:
                terms = [terms[i] + terms[i + 1] for i in range(0, len(terms) - 1, 2)] + terms[len(terms) & ~1 :]
            pending.extend(copies)
            return terms[0]
        return finish

    pending = []
    zeros = jnp.zeros((8, LANES), jnp.float32)

    apply_m(rbuf, zbuf, OFF - 8, (nrow + 16) // 8)
    inner_a(zbuf, OFF - 8, (nrow + 16) // 8)
    outer_a(zbuf, wbuf, OFF - 4, (nrow + 8) // 8, nt)
    total = to_lanes(zeros, 0, gram([(rbuf, zbuf, None)]))
    total = to_lanes(total, groups, gram([(zbuf, wbuf, None)]))
    step0 = post(0, 0, one_row(total))
    apply_m(wbuf, ybuf, OFF - 2, (nrow + 8) // 8)
    step1 = post(1, 0, one_row(to_lanes(zeros, 0, gram([(wbuf, ybuf, None)]))))
    step0 = post(0, 1, step0())
    inner_a(ybuf, OFF - 1, (nrow + 8) // 8)
    step2 = post(2, 0, one_row(to_lanes(zeros, 0, gram([(tbuf, tbuf, 11), (ybuf, ybuf, 10)]))))

    outer_a(ybuf, vbuf, OFF, nrow // 8, nu)
    add = lambda x, y: [a + b for a, b in zip(x, y)]
    minus = lambda x, y: [a - b for a, b in zip(x, y)]

    def keep_coef(m, rows):
        spread = splats(stack_rows(rows, sub), 0)
        for k in range(8):
            for l in range(8):
                coef[m, l, k] = spread[k][l]
        return spread

    def mix(jobs, l0, at_t, u, rows, cols):
        for field, m, base, sign, target in jobs:
            f = [field(k, u, rows, cols) for k in range(8)]
            for l in (l0, l0 + 1):
                total = coef[m, l, 0] * f[0]
                for k in range(1, 8):
                    total = total + coef[m, l, k] * f[k]
                if base is not None:
                    old = base(l, u, rows, cols)
                    total = old + total if sign > 0 else old - total
                elif sign < 0:
                    total = -total
                target[l, at_t, cols] = total

    ext = lambda ref: lambda k, u, rows, cols: ref[u, k, pl.ds(pl.multiple_of(rows + OFF, 8), 8), :]
    flat = lambda ref: lambda k, u, rows, cols: ref[k, pl.ds(pl.multiple_of(rows, 8), 8), cols]

    def mix_all(jobs, l0):
        def body(t, carry):
            for u in range(nu):
                mix(jobs, l0, pl.ds(pl.multiple_of(8 * t, 8), 8), u, 8 * t, slice(u * LANES, (u + 1) * LANES))
            return carry
        lax.fori_loop(0, nrow // 8, body, 0)

    step1 = post(1, 1, step1())
    line0 = step0()
    g1s, g2s = entries(line0, 0), entries(line0, groups)
    g1r, g2r = entry_rows(g1s), entry_rows(g2s)
    alpha = substitute(factor(g2s), g1r)
    alpha_s = keep_coef(0, alpha)
    step2 = post(2, 1, step2())
    for l0 in range(0, PROBES, 2):
        mix_all([(ext(zbuf), 0, None, 1, xs), (ext(wbuf), 0, ext(rbuf), -1, rs),
                 (ext(ybuf), 0, None, -1, ps), (ext(vbuf), 0, None, -1, ws)], l0)
    fact1 = factor(g1s)
    g3s = entries(step1(), 0)
    g3_alpha = product(g3s, alpha)
    gamma = minus(minus(g1r, product(g2s, alpha)), product_t(alpha_s, minus(g2r, g3_alpha)))
    beta = substitute(fact1, gamma)
    eye = [jnp.where(lane == k, 1.0, 0.0) for k in range(8)]
    b_rows = add(beta, eye)
    b_s = keep_coef(1, b_rows)
    part = product_t(b_s, minus(product(g2s, b_rows), g3_alpha))
    g3_b = product(g3s, b_rows)
    for l0 in range(0, PROBES, 2):
        mix_all([(ext(zbuf), 1, flat(ps), 1, ps), (ext(wbuf), 1, flat(ws), 1, ws)], l0)

    g4s = entries(step2(), 0)
    curv = minus(part, product_t(alpha_s, minus(g3_b, product(g4s, alpha))))
    curv_s = splats(stack_rows(curv, sub), 0)
    curv_s = [[0.5 * (curv_s[k][l] + curv_s[l][k]) for l in range(8)] for k in range(8)]
    keep_coef(2, substitute(factor(curv_s), gamma))

    outs = []
    for l in range(PROBES):
        outs.append(pltpu.make_async_copy(xs.at[l], x_out.at[l], osem.at[l]))
        outs.append(pltpu.make_async_copy(rs.at[l], r_out.at[l], osem.at[8 + l]))
    for l0 in range(0, PROBES, 2):
        mix_all([(flat(ps), 2, flat(xs), 1, xs), (flat(ws), 2, flat(rs), -1, rs)], l0)
        for copy in outs[2 * l0 : 2 * l0 + 4]:
            copy.start()
    for copy in pending + col_copies + row_copies:
        copy.wait_send()
    for copy in outs:
        copy.wait()


def shards(probes, kappa_sq, conduct, inv_mass, spai, sea_mask):
    _, nrow, ncol = probes.shape
    rows_n, cols_n = lax.axis_size("row"), lax.axis_size("col")
    nu = ncol // LANES
    nt = nu + 1
    ext = nrow + 2 * OFF
    most = max(2 * cols_n, rows_n // 2)
    f32, bf16 = jnp.float32, jnp.bfloat16
    field = pltpu.VMEM((nt, PROBES, ext, LANES), f32)
    dma = pltpu.SemaphoreType.DMA
    scratch = [
        field, field, field, field, field,
        pltpu.VMEM((25, nrow, ncol), bf16),
        pltpu.VMEM((nt, 25, ext, LANES), f32),
        pltpu.VMEM((nt, 25, ext, LANES), f32),
        pltpu.VMEM((4, nt, ext, LANES), f32),
        pltpu.VMEM((12, nt, ext, LANES), f32),
        pltpu.VMEM((2, 12, HALO, ncol), f32),
        pltpu.VMEM((2, 13, 2 * HALO, ncol), bf16),
        pltpu.VMEM((2, 12, HALO, ncol), f32),
        pltpu.VMEM((2, 13, 2 * HALO, ncol), bf16),
        pltpu.VMEM((nrow, ncol), jnp.int32),
        pltpu.VMEM((2, nrow, LANES), f32),
        pltpu.VMEM((2, nrow, 2 * LANES), bf16),
        pltpu.VMEM((2, nrow + 2 * HALO, LANES), f32),
        pltpu.VMEM((2, ext, 2 * LANES), bf16),
        pltpu.VMEM((3, 2, most, 1, LANES), f32),
        pltpu.VMEM((3, 8, 8, 8, LANES), f32),
        pltpu.VMEM((PROBES, nrow, ncol), f32),
        pltpu.VMEM((PROBES, nrow, ncol), f32),
        pltpu.VMEM((PROBES, nrow, ncol), f32),
        pltpu.VMEM((PROBES, nrow, ncol), f32),
        field,
        dma((2 + 4 * nu,)),
        dma((16,)), dma((16,)),
        dma((3, 2, most)), dma((3, 2, most)),
        dma((16,)),
    ]
    out = jax.ShapeDtypeStruct(probes.shape, f32)
    return pl.pallas_call(
        functools.partial(kernel, nrow, ncol, rows_n, cols_n),
        out_shape=(out, out),
        in_specs=[pl.BlockSpec(memory_space=pl.ANY)] * 6,
        out_specs=(pl.BlockSpec(memory_space=pl.ANY),) * 2,
        scratch_shapes=scratch,
        compiler_params=pltpu.CompilerParams(
            collective_id=0, has_side_effects=True, vmem_limit_bytes=60 * 1024 * 1024),
    )(probes, kappa_sq, conduct, inv_mass, spai, sea_mask)


def solution(mesh):
    field = P(None, "row", "col")
    cell = P("row", "col")
    return jax.shard_map(
        shards, mesh=mesh, in_specs=(field, cell, cell, cell, field, cell),
        out_specs=(field, field), check_vma=False)
```

```python
import functools

import jax
import jax.numpy as jnp
from jax import lax
from jax.experimental import pallas as pl
from jax.experimental.pallas import tpu as pltpu
from jax.sharding import PartitionSpec as P

MESH = pl.DeviceIdType.MESH
PROBES = 8
LANES = 128
HALO = 8
OFF = 16
OFFSETS = [(o // 5 - 2, o % 5 - 2) for o in range(25)]


def tile_shift(tiles, place, step, lane):
    if step == 0:
        return tiles[place]
    count = len(tiles)
    here = pltpu.roll(tiles[place], (-step) % LANES, axis=1)
    if step > 0:
        there = pltpu.roll(tiles[(place + 1) % count], (-step) % LANES, axis=1)
        return jnp.where(lane < LANES - step, here, there)
    there = pltpu.roll(tiles[(place - 1) % count], (-step) % LANES, axis=1)
    return jnp.where(lane >= -step, here, there)


def ring_shifts(tiles, step, lane):
    if step == 0:
        return list(tiles)
    count = len(tiles)
    rolled = [pltpu.roll(tile, (-step) % LANES, axis=1) for tile in tiles]
    if step > 0:
        return [jnp.where(lane < LANES - step, rolled[u], rolled[(u + 1) % count]) for u in range(count)]
    return [jnp.where(lane >= -step, rolled[u], rolled[(u - 1) % count]) for u in range(count)]


def splats(matrix, first):
    out = [[None] * 8 for _ in range(8)]
    for col in range(8):
        wide = jnp.broadcast_to(matrix[:, first + col : first + col + 1], (8, LANES))
        for row in range(8):
            out[row][col] = jnp.broadcast_to(wide[row : row + 1, :], (8, LANES))
    return out


def rows_of(matrix):
    return [jnp.broadcast_to(matrix[k : k + 1, :], (8, LANES)) for k in range(8)]


def stack_rows(rows, sub):
    out = rows[0]
    for k in range(1, 8):
        out = jnp.where(sub == k, rows[k], out)
    return out


def product(left, rows):
    out = []
    for i in range(8):
        total = left[i][0] * rows[0]
        for j in range(1, 8):
            total = total + left[i][j] * rows[j]
        out.append(total)
    return out


def product_t(left, rows):
    return product([[left[j][i] for j in range(8)] for i in range(8)], rows)


def factor(entries):
    a = [list(r) for r in entries]
    mult = [[None] * 8 for _ in range(8)]
    inverse = []
    for j in range(8):
        inv = 1.0 / a[j][j]
        inverse.append(inv)
        for k in range(j + 1, 8):
            mult[k][j] = a[j][k] * inv
            for m in range(k, 8):
                a[k][m] = a[k][m] - mult[k][j] * a[j][m]
    return mult, inverse


def substitute(fact, rows):
    mult, inverse = fact
    y = list(rows)
    for j in range(8):
        for k in range(j + 1, 8):
            y[k] = y[k] - mult[k][j] * y[j]
    y = [y[j] * inverse[j] for j in range(8)]
    for j in range(7, -1, -1):
        for k in range(j):
            y[k] = y[k] - mult[j][k] * y[j]
    return y


def kernel(
    nrow, ncol, rows_n, cols_n,
    probes, kappa, conduct, inv_mass, spai, sea,
    xs, rs,
    rbuf, zbuf, wbuf, ybuf, tbuf, sraw, sfull, symp, cbuf, lap,
    fedge, sedge, fland, sland, seaown, cpack, spack, crecv, srecv,
    grams, coef, ps, ws, vbuf,
    lsem, ssem, rsem, gsend, grecv,
):
    nu = ncol // LANES
    nt = nu + 1
    row = lax.axis_index("row")
    col = lax.axis_index("col")
    core = row % 2
    pair = row // 2
    group1 = 2 * cols_n
    group2 = rows_n // 2
    up, down = (row + rows_n - 1) % rows_n, (row + 1) % rows_n
    left, right = (col + cols_n - 1) % cols_n, (col + 1) % cols_n
    mine1 = core * cols_n + col

    partners1 = []
    for d in range(1, group1):
        q = (mine1 + d) % group1
        partners1.append((row - core + q // cols_n, q % cols_n))
    partners2 = []
    for d in range(1, group2):
        q = (pair + d) % group2
        partners2.append((2 * q + core, col))
    around = [(up, left), (up, col), (up, right), (row, left), (row, right), (down, left), (down, col), (down, right)]

    barrier = pltpu.get_barrier_semaphore()
    for who in around + partners1 + partners2:
        pl.semaphore_signal(barrier, inc=1, device_id=who, device_id_type=MESH)

    local = []
    local.append(pltpu.make_async_copy(spai, sraw, lsem.at[0]))
    for u in range(nu):
        local.append(pltpu.make_async_copy(
            probes.at[:, :, pl.ds(u * LANES, LANES)], rbuf.at[u, :, pl.ds(OFF, nrow), :], lsem.at[1 + u]))
    for k, field in enumerate((kappa, conduct, inv_mass)):
        for u in range(nu):
            local.append(pltpu.make_async_copy(
                field.at[:, pl.ds(u * LANES, LANES)], cbuf.at[k, u, pl.ds(OFF, nrow), :], lsem.at[1 + nu + k * nu + u]))
    local.append(pltpu.make_async_copy(sea, seaown, lsem.at[1 + 4 * nu]))
    for copy in local:
        copy.start()

    lane = lax.broadcasted_iota(jnp.int32, (8, LANES), 1)
    sub = lax.broadcasted_iota(jnp.int32, (8, LANES), 0)
    lane16 = lax.broadcasted_iota(jnp.int32, (16, LANES), 1)
    edge_lanes = jnp.logical_or(lane < HALO, lane >= LANES - HALO)
    edge_lanes16 = jnp.logical_or(lane16 < HALO, lane16 >= LANES - HALO)

    for copy in local[1:]:
        copy.wait()

    def sea_body(t, carry):
        for u in range(nu):
            rows = pl.ds(pl.multiple_of(8 * t, 8), 8)
            dst = pl.ds(pl.multiple_of(OFF + 8 * t, 8), 8)
            cbuf[3, u, dst, :] = seaown[rows, u * LANES : (u + 1) * LANES].astype(jnp.float32)
        return carry
    lax.fori_loop(0, nrow // 8, sea_body, 0)

    for side, at in ((0, OFF + nrow - HALO), (1, OFF)):
        for u in range(nu):
            cols = slice(u * LANES, (u + 1) * LANES)
            for k in range(12):
                fedge[side, k, :, cols] = rbuf[u, k, at : at + 8, :] if k < 8 else cbuf[k - 8, u, at : at + 8, :]

    def pack_body(t, carry):
        src = pl.ds(pl.multiple_of(OFF + 8 * t, 8), 8)
        dst = pl.ds(pl.multiple_of(8 * t, 8), 8)
        group = lane // HALO
        for side, u in ((0, 0), (1, nu - 1)):
            total = jnp.zeros((8, LANES), jnp.float32)
            for k in range(12):
                item = rbuf[u, k, src, :] if k < 8 else cbuf[k - 8, u, src, :]
                moved = pltpu.roll(item, HALO * k, axis=1) if k else item
                total = jnp.where(group == (k - side) % 16, moved, total)
            cpack[side, dst, :] = total
        return carry
    lax.fori_loop(0, nrow // 8, pack_body, 0)

    local[0].wait()

    for side, at16, skip in ((0, nrow - 16, 8), (1, 0, 0)):
        for u in range(nu):
            cols = slice(u * LANES, (u + 1) * LANES)
            for j in range(13):
                first = sraw[2 * j, at16 : at16 + 16, cols].astype(jnp.float32)[skip : skip + 8]
                second = sraw[min(2 * j + 1, 24), at16 : at16 + 16, cols].astype(jnp.float32)[skip : skip + 8]
                sedge[side, j, :, cols] = jnp.concatenate([first, second], axis=0).astype(jnp.bfloat16)

    pl.semaphore_wait(barrier, len(around) + len(partners1) + len(partners2))

    def remote(index, src, dst, who):
        return pltpu.make_async_remote_copy(
            src_ref=src, dst_ref=dst, send_sem=ssem.at[index], recv_sem=rsem.at[index],
            device_id=who, device_id_type=MESH)

    row_copies = []
    for side, who in ((0, down), (1, up)):
        row_copies.append(remote(2 * side, sedge.at[side], sland.at[side], (who, col)))
        row_copies.append(remote(2 * side + 1, fedge.at[side], fland.at[side], (who, col)))
    col_copies = []
    for side, who in ((0, left), (1, right)):
        to = 1 - side
        base = 4 + 6 * side
        col_copies += [
            remote(base, spack.at[side, pl.ds(0, OFF), :], srecv.at[to, pl.ds(OFF + nrow, OFF), :], (up, who)),
            remote(base + 1, cpack.at[side, pl.ds(0, HALO), :], crecv.at[to, pl.ds(HALO + nrow, HALO), :], (up, who)),
            remote(base + 2, spack.at[side, pl.ds(nrow - OFF, OFF), :], srecv.at[to, pl.ds(0, OFF), :], (down, who)),
            remote(base + 3, cpack.at[side, pl.ds(nrow - HALO, HALO), :], crecv.at[to, pl.ds(0, HALO), :], (down, who)),
            remote(base + 4, spack.at[side], srecv.at[to, pl.ds(OFF, nrow), :], (row, who)),
            remote(base + 5, cpack.at[side], crecv.at[to, pl.ds(HALO, nrow), :], (row, who)),
        ]
    for copy in row_copies:
        copy.start()
    direct = [copy for k, copy in enumerate(col_copies) if k % 6 >= 4]
    corners = [copy for k, copy in enumerate(col_copies) if k % 6 < 4]
    for copy in direct[1::2] + corners[1::2]:
        copy.start()

    def spack_body(t, carry):
        src = pl.ds(pl.multiple_of(16 * t, 16), 16)
        full = pl.ds(pl.multiple_of(OFF + 16 * t, 16), 16)
        group = lane16 // HALO
        for o in range(25):
            tiles = []
            for u in range(nu):
                tile = sraw[o, src, u * LANES : (u + 1) * LANES].astype(jnp.float32)
                sfull[u, o, full, :] = tile
                tiles.append(tile)
            if o % 16 == 0:
                totals = [jnp.zeros((16, LANES), jnp.float32)] * 2
            for side, u in ((0, 0), (1, nu - 1)):
                shift = (HALO * o) % LANES
                moved = pltpu.roll(tiles[u], shift, axis=1) if shift else tiles[u]
                totals[side] = jnp.where(group == (o - side) % 16, moved, totals[side])
            if o % 16 == 15 or o == 24:
                part = o // 16
                for side in range(2):
                    spack[side, src, part * LANES : (part + 1) * LANES] = totals[side].astype(jnp.bfloat16)
        return carry
    lax.fori_loop(0, nrow // 16, spack_body, 0)

    for copy in direct[0::2] + corners[0::2]:
        copy.start()

    one = jnp.float32(1.0)
    zero = jnp.float32(0.0)
    has_up = jnp.where(row > 0, one, zero)
    has_down = jnp.where(row < rows_n - 1, one, zero)
    has_left = jnp.where(col > 0, one, zero)
    has_right = jnp.where(col < cols_n - 1, one, zero)

    def rotate_body(t, carry):
        here = pl.ds(pl.multiple_of(OFF + 8 * t, 8), 8)
        for o, (a, b) in enumerate(OFFSETS):
            if b:
                for u in range(nu):
                    symp[u, o, here, :] = pltpu.roll(sfull[u, o, here, :], b % LANES, axis=1)
        return carry
    lax.fori_loop(0, nrow // 8, rotate_body, 0)

    def inside_rows(first, sublane):
        at = first + sublane
        above = jnp.where(at < OFF, has_up, one)
        return jnp.where(at >= OFF + nrow, has_down, above)

    def unpack_body(t, carry):
        src = pl.ds(pl.multiple_of(8 * t, 8), 8)
        dst = pl.ds(pl.multiple_of(OFF - HALO + 8 * t, 8), 8)
        rowmask = inside_rows(OFF - HALO + 8 * t, sub)
        from_left = crecv[0, src, :] * (rowmask * has_left)
        from_right = crecv[1, src, :] * (rowmask * has_right)
        odd = (lane // HALO) % 2 == 1
        merged = (jnp.where(odd, from_left, from_right), jnp.where(odd, from_right, from_left))
        for k in range(12):
            moved = pltpu.roll(merged[k % 2], (-HALO * k) % LANES, axis=1) if k else merged[0]
            tile = jnp.where(edge_lanes, moved, 0.0)
            if k < 8:
                rbuf[nu, k, dst, :] = tile
            else:
                cbuf[k - 8, nu, dst, :] = tile
        return carry

    def sunpack_body(t, carry):
        src = pl.ds(pl.multiple_of(16 * t, 16), 16)
        rowmask = inside_rows(16 * t, lax.broadcasted_iota(jnp.int32, (16, LANES), 0))
        for part in range(2):
            cols = slice(part * LANES, (part + 1) * LANES)
            from_left = srecv[0, src, cols].astype(jnp.float32) * (rowmask * has_left)
            from_right = srecv[1, src, cols].astype(jnp.float32) * (rowmask * has_right)
            odd = (lane16 // HALO) % 2 == 1
            merged = (jnp.where(odd, from_left, from_right), jnp.where(odd, from_right, from_left))
            for k in range(16 if part == 0 else 9):
                moved = pltpu.roll(merged[k % 2], (-HALO * k) % LANES, axis=1) if k else merged[0]
                sfull[nu, 16 * part + k, src, :] = jnp.where(edge_lanes16, moved, 0.0)
        return carry

    colmask = [jnp.ones((8, LANES), jnp.float32)] * nu + [
        jnp.where(lane < LANES // 2, has_right, has_left)]

    def sym_tile(at, rotated):
        here = pl.ds(at, 8)
        rowmask = inside_rows(at, sub) * 0.5
        masks = {b: ring_shifts([m * rowmask for m in colmask], -b, lane) for b in range(-2, 3)}
        for o, (a, b) in enumerate(OFFSETS):
            if b == 0:
                own = [sfull[u, o, here, :] for u in range(nt)]
            else:
                rolled = [
                    symp[u, o, here, :] if rotated and u < nu else pltpu.roll(sfull[u, o, here, :], b % LANES, axis=1)
                    for u in range(nt)]
                if b < 0:
                    own = [jnp.where(lane < LANES + b, rolled[u], rolled[(u + 1) % nt]) for u in range(nt)]
                else:
                    own = [jnp.where(lane >= b, rolled[u], rolled[(u - 1) % nt]) for u in range(nt)]
            for u in range(nt):
                mirror = sfull[u, 24 - o, pl.ds(at + a, 8), :]
                symp[u, o, here, :] = (own[u] + mirror) * masks[b][u]

    inner_tiles = nrow // 8 - 2
    inner_at = lambda t: pl.multiple_of(OFF + 8 + 8 * t, 8)
    rim_at = lambda t: pl.multiple_of(OFF - HALO + 8 * t + (t // 2) * 8 * inner_tiles, 8)
    edge_at = lambda t: pl.multiple_of(OFF + t * (nrow - 8), 8)
    halo_at = lambda t: pl.multiple_of(OFF - HALO + t * (nrow + HALO), 8)

    def each(count, place, body):
        def step(t, carry):
            body(place(t))
            return carry
        lax.fori_loop(0, count, step, 0)

    def lap_tile(at):
        here = pl.ds(at, 8)
        above, below = pl.ds(at - 1, 8), pl.ds(at + 1, 8)
        tiles = lambda k, rows: [cbuf[k, u, rows, :] for u in range(nt)]
        kap, con, inv, msk = (tiles(k, here) for k in range(4))
        con_n = ring_shifts(con, 1, lane)
        east = [0.5 * (con[u] + con_n[u]) for u in range(nt)]
        west = ring_shifts(east, -1, lane)
        inv_e, inv_w = ring_shifts(inv, 1, lane), ring_shifts(inv, -1, lane)
        msk_e, msk_w = ring_shifts(msk, 1, lane), ring_shifts(msk, -1, lane)
        for u in range(nt):
            north = 0.5 * (con[u] + cbuf[1, u, above, :])
            south = 0.5 * (con[u] + cbuf[1, u, below, :])
            diag = kap[u] + north + south + west[u] + east[u]
            lap[0, u, here, :] = inv[u] * diag * msk[u]
            lap[1, u, here, :] = inv[u] * north * cbuf[3, u, above, :]
            lap[2, u, here, :] = inv[u] * south * cbuf[3, u, below, :]
            lap[3, u, here, :] = inv_w[u] * west[u] * msk[u]
            lap[4, u, here, :] = inv_e[u] * east[u] * msk[u]
            lap[5, u, here, :] = msk[u] * diag
            lap[6, u, here, :] = msk[u] * north
            lap[7, u, here, :] = msk[u] * south
            lap[8, u, here, :] = msk_w[u] * west[u]
            lap[9, u, here, :] = msk_e[u] * east[u]
            lap[10, u, here, :] = 1.0 - msk[u]
            if u < nu:
                lap[11, u, here, :] = 1.0 / inv[u]

    def apply_m(src, dst, place, count):
        def body(at):
            for p0 in range(0, PROBES, 2):
                pair_p = (p0, p0 + 1)
                field = {(p, a, u): src[u, p, pl.ds(at + a, 8), :] for p in pair_p for a in range(-2, 3) for u in range(nt)}
                total = {}
                for b in range(-2, 3):
                    part = {}
                    for a in range(-2, 3):
                        o = (a + 2) * 5 + b + 2
                        for u in range(nt):
                            weight = symp[u, o, pl.ds(at, 8), :]
                            for p in pair_p:
                                term = weight * field[p, a, u]
                                part[p, u] = term if a == -2 else part[p, u] + term
                    for p in pair_p:
                        moved = ring_shifts([part[p, u] for u in range(nt)], b, lane)
                        for u in range(nt):
                            total[p, u] = moved[u] if b == -2 else total[p, u] + moved[u]
                for p in pair_p:
                    for u in range(nt):
                        dst[u, p, pl.ds(at, 8), :] = total[p, u]
        each(count, place, body)

    def half_laplace(first, src, at, p, coefs):
        centre = [src[u, p, pl.ds(at, 8), :] for u in range(nt)]
        to_east = ring_shifts([coefs[3][u] * centre[u] for u in range(nt)], 1, lane)
        to_west = ring_shifts([coefs[4][u] * centre[u] for u in range(nt)], -1, lane)
        out = []
        for u in range(nt):
            across = to_east[u] + to_west[u]
            along = coefs[1][u] * src[u, p, pl.ds(at - 1, 8), :] + coefs[2][u] * src[u, p, pl.ds(at + 1, 8), :]
            out.append(coefs[0][u] * centre[u] - (across + along))
        return out

    def inner_a(src, start, count):
        def body(t, carry):
            at = start + 8 * t
            coefs = [[lap[k, u, pl.ds(at, 8), :] for u in range(nt)] for k in range(5)]
            for p in range(PROBES):
                out = half_laplace(0, src, at, p, coefs)
                for u in range(nt):
                    tbuf[u, p, pl.ds(at, 8), :] = out[u]
            return carry
        lax.fori_loop(0, count, body, 0)

    def outer_a(src, dst, start, count, keep):
        def body(t, carry):
            at = start + 8 * t
            coefs = [[lap[5 + k, u, pl.ds(at, 8), :] for u in range(nt)] for k in range(6)]
            for p in range(PROBES):
                out = half_laplace(5, tbuf, at, p, coefs)
                for u in range(keep):
                    dst[u, p, pl.ds(at, 8), :] = out[u] + coefs[5][u] * src[u, p, pl.ds(at, 8), :]
            return carry
        lax.fori_loop(0, count, body, 0)

    pairs = [(k, l) for k in range(8) for l in range(k, 8)]

    groups = -(-len(pairs) // 8)

    def gram(terms):
        def body(i, acc):
            u = i // (nrow // 8)
            rows = pl.ds(pl.multiple_of(OFF + 8 * (i % (nrow // 8)), 8), 8)
            for first, second, weight in terms:
                a = [first[u, p, rows, :] for p in range(PROBES)]
                if weight is not None:
                    w = lap[weight, u, rows, :]
                    a = [w * x for x in a]
                b = [second[u, p, rows, :] for p in range(PROBES)]
                acc = tuple(acc[n] + a[k] * b[l] for n, (k, l) in enumerate(pairs))
            return acc
        start = tuple(jnp.zeros((8, LANES), jnp.float32) for _ in pairs)
        return lax.fori_loop(0, nu * (nrow // 8), body, start)

    def to_lanes(total, first, acc):
        for j in range(groups):
            stacked = None
            for s in range(8):
                if 8 * j + s < len(acc):
                    entry = jnp.broadcast_to(jnp.sum(acc[8 * j + s], axis=0, keepdims=True), (8, LANES))
                    stacked = entry if stacked is None else jnp.where(sub == s, entry, stacked)
            total = jnp.where(lane == first + j, jnp.sum(stacked, axis=1, keepdims=True), total)
        return total

    def one_row(total):
        spread = pltpu.roll(total, 0, axis=1, stride=16, stride_axis=0)
        return jnp.sum(spread, axis=0, keepdims=True)

    def entries(line, first):
        out = [[None] * 8 for _ in range(8)]
        for n, (k, l) in enumerate(pairs):
            at = 16 * (n % 8) + first + n // 8
            out[k][l] = out[l][k] = jnp.broadcast_to(line[:, at : at + 1], (8, LANES))
        return out

    def entry_rows(spread):
        out = []
        for k in range(8):
            line = spread[k][0]
            for l in range(1, 8):
                line = jnp.where(lane == l, spread[k][l], line)
            out.append(line)
        return out

    def post(step, phase, value):
        mine, partners, count = ((mine1, partners1, group1), (pair, partners2, group2))[phase]
        buf = grams.at[step, phase]
        buf[mine] = value
        copies = [pltpu.make_async_remote_copy(
            src_ref=buf.at[mine], dst_ref=buf.at[mine],
            send_sem=gsend.at[step, phase, d], recv_sem=grecv.at[step, phase, mine],
            device_id=who, device_id_type=MESH) for d, who in enumerate(partners)]
        for copy in copies:
            copy.start()

        def finish():
            for d in range(1, count):
                slot = (mine + d) % count
                pltpu.make_async_copy(buf.at[slot], buf.at[slot], grecv.at[step, phase, slot]).wait()
            terms = [buf[k] for k in range(count)]
            while len(terms) > 1:
                terms = [terms[i] + terms[i + 1] for i in range(0, len(terms) - 1, 2)] + terms[len(terms) & ~1 :]
            pending.extend(copies)
            return terms[0]
        return finish

    pending = []
    zeros = jnp.zeros((8, LANES), jnp.float32)

    for copy in direct:
        copy.wait_recv()
    lax.fori_loop(1, nrow // 8 + 1, unpack_body, 0)
    each(inner_tiles, inner_at, lap_tile)
    lax.fori_loop(1, nrow // 16 + 1, sunpack_body, 0)
    each(inner_tiles, inner_at, lambda at: sym_tile(at, True))
    apply_m(rbuf, zbuf, inner_at, inner_tiles)
    for copy in row_copies:
        copy.wait_recv()
    for side, keep, at in ((0, has_up, OFF - HALO), (1, has_down, OFF + nrow)):
        for u in range(nu):
            cols = slice(u * LANES, (u + 1) * LANES)
            for k in range(12):
                item = fland[side, k, :, cols] * keep
                if k < 8:
                    rbuf[u, k, at : at + 8, :] = item
                else:
                    cbuf[k - 8, u, at : at + 8, :] = item
            for j in range(13):
                both = sland[side, j, :, cols].astype(jnp.float32) * keep
                sfull[u, 2 * j, at : at + 8, :] = both[0:8]
                if j < 12:
                    sfull[u, 2 * j + 1, at : at + 8, :] = both[8:16]

    for copy in corners:
        copy.wait_recv()
    lax.fori_loop(0, 2, lambda t, carry: unpack_body(t * (nrow // 8 + 1), carry), 0)
    lax.fori_loop(0, 2, lambda t, carry: sunpack_body(t * (nrow // 16 + 1), carry), 0)
    each(4, rim_at, lap_tile)
    each(2, edge_at, lambda at: sym_tile(at, True))
    each(2, halo_at, lambda at: sym_tile(at, False))
    apply_m(rbuf, zbuf, rim_at, 4)
    inner_a(zbuf, OFF - 8, (nrow + 16) // 8)
    outer_a(zbuf, wbuf, OFF - 4, (nrow + 8) // 8, nt)
    total = to_lanes(zeros, 0, gram([(rbuf, zbuf, None)]))
    total = to_lanes(total, groups, gram([(zbuf, wbuf, None)]))
    step0 = post(0, 0, one_row(total))
    apply_m(wbuf, ybuf, lambda t: OFF - 2 + 8 * t, (nrow + 8) // 8)
    step1 = post(1, 0, one_row(to_lanes(zeros, 0, gram([(wbuf, ybuf, None)]))))
    step0 = post(0, 1, step0())
    inner_a(ybuf, OFF - 1, (nrow + 8) // 8)
    step2 = post(2, 0, one_row(to_lanes(zeros, 0, gram([(tbuf, tbuf, 11), (ybuf, ybuf, 10)]))))

    outer_a(ybuf, vbuf, OFF, nrow // 8, nu)
    add = lambda x, y: [a + b for a, b in zip(x, y)]
    minus = lambda x, y: [a - b for a, b in zip(x, y)]

    def keep_coef(m, rows):
        spread = splats(stack_rows(rows, sub), 0)
        for k in range(8):
            for l in range(8):
                coef[m, l, k] = spread[k][l]
        return spread

    def mix(jobs, l0, at_t, u, rows, cols):
        for field, m, base, sign, target in jobs:
            f = [field(k, u, rows, cols) for k in range(8)]
            for l in (l0, l0 + 1):
                total = coef[m, l, 0] * f[0]
                for k in range(1, 8):
                    total = total + coef[m, l, k] * f[k]
                if base is not None:
                    old = base(l, u, rows, cols)
                    total = old + total if sign > 0 else old - total
                elif sign < 0:
                    total = -total
                target[l, at_t, cols] = total

    ext = lambda ref: lambda k, u, rows, cols: ref[u, k, pl.ds(pl.multiple_of(rows + OFF, 8), 8), :]
    flat = lambda ref: lambda k, u, rows, cols: ref[k, pl.ds(pl.multiple_of(rows, 8), 8), cols]

    def mix_all(jobs, l0):
        def body(t, carry):
            for u in range(nu):
                mix(jobs, l0, pl.ds(pl.multiple_of(8 * t, 8), 8), u, 8 * t, slice(u * LANES, (u + 1) * LANES))
            return carry
        lax.fori_loop(0, nrow // 8, body, 0)

    step1 = post(1, 1, step1())
    line0 = step0()
    g1s, g2s = entries(line0, 0), entries(line0, groups)
    g1r, g2r = entry_rows(g1s), entry_rows(g2s)
    alpha = substitute(factor(g2s), g1r)
    alpha_s = keep_coef(0, alpha)
    step2 = post(2, 1, step2())
    for l0 in range(0, PROBES, 2):
        mix_all([(ext(zbuf), 0, None, 1, xs), (ext(wbuf), 0, ext(rbuf), -1, rs),
                 (ext(ybuf), 0, None, -1, ps), (ext(vbuf), 0, None, -1, ws)], l0)
    fact1 = factor(g1s)
    g3s = entries(step1(), 0)
    g3_alpha = product(g3s, alpha)
    gamma = minus(minus(g1r, product(g2s, alpha)), product_t(alpha_s, minus(g2r, g3_alpha)))
    beta = substitute(fact1, gamma)
    eye = [jnp.where(lane == k, 1.0, 0.0) for k in range(8)]
    b_rows = add(beta, eye)
    b_s = keep_coef(1, b_rows)
    part = product_t(b_s, minus(product(g2s, b_rows), g3_alpha))
    g3_b = product(g3s, b_rows)
    for l0 in range(0, PROBES, 2):
        mix_all([(ext(zbuf), 1, flat(ps), 1, ps), (ext(wbuf), 1, flat(ws), 1, ws)], l0)

    g4s = entries(step2(), 0)
    curv = minus(part, product_t(alpha_s, minus(g3_b, product(g4s, alpha))))
    curv_s = splats(stack_rows(curv, sub), 0)
    curv_s = [[0.5 * (curv_s[k][l] + curv_s[l][k]) for l in range(8)] for k in range(8)]
    keep_coef(2, substitute(factor(curv_s), gamma))

    for l0 in range(0, PROBES, 2):
        mix_all([(flat(ps), 2, flat(xs), 1, xs), (flat(ws), 2, flat(rs), -1, rs)], l0)
    for copy in pending + col_copies + row_copies:
        copy.wait_send()


def copy_kernel(x_in, r_in, x_out, r_out, sem):
    copies = []
    for p in range(0, PROBES, 2):
        two = pl.ds(p, 2)
        copies.append(pltpu.make_async_copy(x_in.at[two], x_out.at[two], sem.at[p]))
        copies.append(pltpu.make_async_copy(r_in.at[two], r_out.at[two], sem.at[p + 1]))
    for copy in copies:
        copy.start()
    for copy in copies:
        copy.wait()


def shards(probes, kappa_sq, conduct, inv_mass, spai, sea_mask):
    _, nrow, ncol = probes.shape
    rows_n, cols_n = lax.axis_size("row"), lax.axis_size("col")
    nu = ncol // LANES
    nt = nu + 1
    ext = nrow + 2 * OFF
    most = max(2 * cols_n, rows_n // 2)
    f32, bf16 = jnp.float32, jnp.bfloat16
    field = pltpu.VMEM((nt, PROBES, ext, LANES), f32)
    dma = pltpu.SemaphoreType.DMA
    scratch = [
        field, field, field, field, field,
        pltpu.VMEM((25, nrow, ncol), bf16),
        pltpu.VMEM((nt, 25, ext, LANES), f32),
        pltpu.VMEM((nt, 25, ext, LANES), f32),
        pltpu.VMEM((4, nt, ext, LANES), f32),
        pltpu.VMEM((12, nt, ext, LANES), f32),
        pltpu.VMEM((2, 12, HALO, ncol), f32),
        pltpu.VMEM((2, 13, 2 * HALO, ncol), bf16),
        pltpu.VMEM((2, 12, HALO, ncol), f32),
        pltpu.VMEM((2, 13, 2 * HALO, ncol), bf16),
        pltpu.VMEM((nrow, ncol), jnp.int32),
        pltpu.VMEM((2, nrow, LANES), f32),
        pltpu.VMEM((2, nrow, 2 * LANES), bf16),
        pltpu.VMEM((2, nrow + 2 * HALO, LANES), f32),
        pltpu.VMEM((2, ext, 2 * LANES), bf16),
        pltpu.VMEM((3, 2, most, 1, LANES), f32),
        pltpu.VMEM((3, 8, 8, 8, LANES), f32),
        pltpu.VMEM((PROBES, nrow, ncol), f32),
        pltpu.VMEM((PROBES, nrow, ncol), f32),
        field,
        dma((2 + 4 * nu,)),
        dma((16,)), dma((16,)),
        dma((3, 2, most)), dma((3, 2, most)),
    ]
    out = jax.ShapeDtypeStruct(probes.shape, f32)
    hbm = pl.BlockSpec(memory_space=pl.ANY)
    parts = pl.pallas_call(
        functools.partial(kernel, nrow, ncol, rows_n, cols_n),
        out_shape=(pltpu.VMEM(probes.shape, f32),) * 2,
        in_specs=[pl.BlockSpec(memory_space=pltpu.HBM)] * 6,
        out_specs=(pl.BlockSpec(memory_space=pltpu.VMEM),) * 2,
        scratch_shapes=scratch,
        compiler_params=pltpu.CompilerParams(
            collective_id=0, has_side_effects=True, vmem_limit_bytes=48 * 1024 * 1024),
    )(*[pltpu.with_memory_space_constraint(v, pltpu.HBM) for v in (probes, kappa_sq, conduct, inv_mass, spai, sea_mask)])
    return pl.pallas_call(
        copy_kernel,
        out_shape=(out, out),
        in_specs=[hbm] * 2,
        out_specs=(pl.BlockSpec(memory_space=pltpu.HBM),) * 2,
        scratch_shapes=[dma((8,))],
        compiler_params=pltpu.CompilerParams(vmem_limit_bytes=16 * 1024 * 1024),
    )(*parts)


def solution(mesh):
    field = P(None, "row", "col")
    cell = P("row", "col")
    return jax.shard_map(
        shards, mesh=mesh, in_specs=(field, cell, cell, cell, field, cell),
        out_specs=(field, field), check_vma=False)
```

```python
import functools

import jax
import jax.numpy as jnp
from jax import lax
from jax.experimental import pallas as pl
from jax.experimental.pallas import tpu as pltpu
from jax.sharding import PartitionSpec as P

MESH = pl.DeviceIdType.MESH
PROBES = 8
LANES = 128
HALO = 8
OFF = 16
OFFSETS = [(o // 5 - 2, o % 5 - 2) for o in range(25)]


def tile_shift(tiles, place, step, lane):
    if step == 0:
        return tiles[place]
    count = len(tiles)
    here = pltpu.roll(tiles[place], (-step) % LANES, axis=1)
    if step > 0:
        there = pltpu.roll(tiles[(place + 1) % count], (-step) % LANES, axis=1)
        return jnp.where(lane < LANES - step, here, there)
    there = pltpu.roll(tiles[(place - 1) % count], (-step) % LANES, axis=1)
    return jnp.where(lane >= -step, here, there)


def ring_shifts(tiles, step, lane):
    if step == 0:
        return list(tiles)
    count = len(tiles)
    rolled = [pltpu.roll(tile, (-step) % LANES, axis=1) for tile in tiles]
    if step > 0:
        return [jnp.where(lane < LANES - step, rolled[u], rolled[(u + 1) % count]) for u in range(count)]
    return [jnp.where(lane >= -step, rolled[u], rolled[(u - 1) % count]) for u in range(count)]


def splats(matrix, first):
    out = [[None] * 8 for _ in range(8)]
    for col in range(8):
        wide = jnp.broadcast_to(matrix[:, first + col : first + col + 1], (8, LANES))
        for row in range(8):
            out[row][col] = jnp.broadcast_to(wide[row : row + 1, :], (8, LANES))
    return out


def rows_of(matrix):
    return [jnp.broadcast_to(matrix[k : k + 1, :], (8, LANES)) for k in range(8)]


def stack_rows(rows, sub):
    out = rows[0]
    for k in range(1, 8):
        out = jnp.where(sub == k, rows[k], out)
    return out


def product(left, rows):
    out = []
    for i in range(8):
        total = left[i][0] * rows[0]
        for j in range(1, 8):
            total = total + left[i][j] * rows[j]
        out.append(total)
    return out


def product_t(left, rows):
    return product([[left[j][i] for j in range(8)] for i in range(8)], rows)


def factor(entries):
    a = [list(r) for r in entries]
    mult = [[None] * 8 for _ in range(8)]
    inverse = []
    for j in range(8):
        inv = 1.0 / a[j][j]
        inverse.append(inv)
        for k in range(j + 1, 8):
            mult[k][j] = a[j][k] * inv
            for m in range(k, 8):
                a[k][m] = a[k][m] - mult[k][j] * a[j][m]
    return mult, inverse


def substitute(fact, rows):
    mult, inverse = fact
    y = list(rows)
    for j in range(8):
        for k in range(j + 1, 8):
            y[k] = y[k] - mult[k][j] * y[j]
    y = [y[j] * inverse[j] for j in range(8)]
    for j in range(7, -1, -1):
        for k in range(j):
            y[k] = y[k] - mult[j][k] * y[j]
    return y


def kernel(
    nrow, ncol, rows_n, cols_n,
    probes, kappa, conduct, inv_mass, spai, sea,
    xs, rs,
    rbuf, zbuf, wbuf, ybuf, tbuf, sraw, sfull, symp, cbuf, lap,
    fedge, sedge, fland, sland, seaown, cpack, spack, crecv, srecv,
    grams, coef, ps, ws, vbuf,
    lsem, ssem, rsem, gsend, grecv,
):
    nu = ncol // LANES
    nt = nu + 1
    row = lax.axis_index("row")
    col = lax.axis_index("col")
    core = row % 2
    pair = row // 2
    group1 = 2 * cols_n
    group2 = rows_n // 2
    up, down = (row + rows_n - 1) % rows_n, (row + 1) % rows_n
    left, right = (col + cols_n - 1) % cols_n, (col + 1) % cols_n
    mine1 = core * cols_n + col

    partners1 = []
    for d in range(1, group1):
        q = (mine1 + d) % group1
        partners1.append((row - core + q // cols_n, q % cols_n))
    partners2 = []
    for d in range(1, group2):
        q = (pair + d) % group2
        partners2.append((2 * q + core, col))
    around = [(up, left), (up, col), (up, right), (row, left), (row, right), (down, left), (down, col), (down, right)]

    barrier = pltpu.get_barrier_semaphore()
    for who in around + partners1 + partners2:
        pl.semaphore_signal(barrier, inc=1, device_id=who, device_id_type=MESH)

    local = []
    local.append(pltpu.make_async_copy(spai, sraw, lsem.at[0]))
    for u in range(nu):
        local.append(pltpu.make_async_copy(
            probes.at[:, :, pl.ds(u * LANES, LANES)], rbuf.at[u, :, pl.ds(OFF, nrow), :], lsem.at[1 + u]))
    for k, field in enumerate((kappa, conduct, inv_mass)):
        for u in range(nu):
            local.append(pltpu.make_async_copy(
                field.at[:, pl.ds(u * LANES, LANES)], cbuf.at[k, u, pl.ds(OFF, nrow), :], lsem.at[1 + nu + k * nu + u]))
    local.append(pltpu.make_async_copy(sea, seaown, lsem.at[1 + 4 * nu]))
    for copy in local:
        copy.start()

    lane = lax.broadcasted_iota(jnp.int32, (8, LANES), 1)
    sub = lax.broadcasted_iota(jnp.int32, (8, LANES), 0)
    lane16 = lax.broadcasted_iota(jnp.int32, (16, LANES), 1)
    edge_lanes = jnp.logical_or(lane < HALO, lane >= LANES - HALO)
    edge_lanes16 = jnp.logical_or(lane16 < HALO, lane16 >= LANES - HALO)

    for copy in local[1:]:
        copy.wait()

    def sea_body(t, carry):
        for u in range(nu):
            rows = pl.ds(pl.multiple_of(8 * t, 8), 8)
            dst = pl.ds(pl.multiple_of(OFF + 8 * t, 8), 8)
            cbuf[3, u, dst, :] = seaown[rows, u * LANES : (u + 1) * LANES].astype(jnp.float32)
        return carry
    lax.fori_loop(0, nrow // 8, sea_body, 0)

    for side, at in ((0, OFF + nrow - HALO), (1, OFF)):
        for u in range(nu):
            cols = slice(u * LANES, (u + 1) * LANES)
            for k in range(12):
                fedge[side, k, :, cols] = rbuf[u, k, at : at + 8, :] if k < 8 else cbuf[k - 8, u, at : at + 8, :]

    def pack_body(t, carry):
        src = pl.ds(pl.multiple_of(OFF + 8 * t, 8), 8)
        dst = pl.ds(pl.multiple_of(8 * t, 8), 8)
        group = lane // HALO
        for side, u in ((0, 0), (1, nu - 1)):
            total = jnp.zeros((8, LANES), jnp.float32)
            for k in range(12):
                item = rbuf[u, k, src, :] if k < 8 else cbuf[k - 8, u, src, :]
                moved = pltpu.roll(item, HALO * k, axis=1) if k else item
                total = jnp.where(group == (k - side) % 16, moved, total)
            cpack[side, dst, :] = total
        return carry
    lax.fori_loop(0, nrow // 8, pack_body, 0)

    local[0].wait()

    for side, at16, skip in ((0, nrow - 16, 8), (1, 0, 0)):
        for u in range(nu):
            cols = slice(u * LANES, (u + 1) * LANES)
            for j in range(13):
                first = sraw[2 * j, at16 : at16 + 16, cols].astype(jnp.float32)[skip : skip + 8]
                second = sraw[min(2 * j + 1, 24), at16 : at16 + 16, cols].astype(jnp.float32)[skip : skip + 8]
                sedge[side, j, :, cols] = jnp.concatenate([first, second], axis=0).astype(jnp.bfloat16)

    pl.semaphore_wait(barrier, len(around) + len(partners1) + len(partners2))

    def remote(index, src, dst, who):
        return pltpu.make_async_remote_copy(
            src_ref=src, dst_ref=dst, send_sem=ssem.at[index], recv_sem=rsem.at[index],
            device_id=who, device_id_type=MESH)

    row_copies = []
    for side, who in ((0, down), (1, up)):
        row_copies.append(remote(2 * side, sedge.at[side], sland.at[side], (who, col)))
        row_copies.append(remote(2 * side + 1, fedge.at[side], fland.at[side], (who, col)))
    col_copies = []
    for side, who in ((0, left), (1, right)):
        to = 1 - side
        base = 4 + 6 * side
        col_copies += [
            remote(base, spack.at[side, pl.ds(0, OFF), :], srecv.at[to, pl.ds(OFF + nrow, OFF), :], (up, who)),
            remote(base + 1, cpack.at[side, pl.ds(0, HALO), :], crecv.at[to, pl.ds(HALO + nrow, HALO), :], (up, who)),
            remote(base + 2, spack.at[side, pl.ds(nrow - OFF, OFF), :], srecv.at[to, pl.ds(0, OFF), :], (down, who)),
            remote(base + 3, cpack.at[side, pl.ds(nrow - HALO, HALO), :], crecv.at[to, pl.ds(0, HALO), :], (down, who)),
            remote(base + 4, spack.at[side], srecv.at[to, pl.ds(OFF, nrow), :], (row, who)),
            remote(base + 5, cpack.at[side], crecv.at[to, pl.ds(HALO, nrow), :], (row, who)),
        ]
    for copy in row_copies:
        copy.start()
    direct = [copy for k, copy in enumerate(col_copies) if k % 6 >= 4]
    corners = [copy for k, copy in enumerate(col_copies) if k % 6 < 4]
    for copy in direct[1::2] + corners[1::2]:
        copy.start()

    def spack_body(t, carry):
        src = pl.ds(pl.multiple_of(16 * t, 16), 16)
        full = pl.ds(pl.multiple_of(OFF + 16 * t, 16), 16)
        group = lane16 // HALO
        for o in range(25):
            tiles = []
            for u in range(nu):
                tile = sraw[o, src, u * LANES : (u + 1) * LANES].astype(jnp.float32)
                sfull[u, o, full, :] = tile
                tiles.append(tile)
            if o % 16 == 0:
                totals = [jnp.zeros((16, LANES), jnp.float32)] * 2
            for side, u in ((0, 0), (1, nu - 1)):
                shift = (HALO * o) % LANES
                moved = pltpu.roll(tiles[u], shift, axis=1) if shift else tiles[u]
                totals[side] = jnp.where(group == (o - side) % 16, moved, totals[side])
            if o % 16 == 15 or o == 24:
                part = o // 16
                for side in range(2):
                    spack[side, src, part * LANES : (part + 1) * LANES] = totals[side].astype(jnp.bfloat16)
        return carry
    lax.fori_loop(0, nrow // 16, spack_body, 0)

    for copy in direct[0::2] + corners[0::2]:
        copy.start()

    one = jnp.float32(1.0)
    zero = jnp.float32(0.0)
    has_up = jnp.where(row > 0, one, zero)
    has_down = jnp.where(row < rows_n - 1, one, zero)
    has_left = jnp.where(col > 0, one, zero)
    has_right = jnp.where(col < cols_n - 1, one, zero)

    def rotate_body(t, carry):
        here = pl.ds(pl.multiple_of(OFF + 8 * t, 8), 8)
        for o, (a, b) in enumerate(OFFSETS):
            if b:
                for u in range(nu):
                    symp[u, o, here, :] = pltpu.roll(sfull[u, o, here, :], b % LANES, axis=1)
        return carry
    lax.fori_loop(0, nrow // 8, rotate_body, 0)

    def inside_rows(first, sublane):
        at = first + sublane
        above = jnp.where(at < OFF, has_up, one)
        return jnp.where(at >= OFF + nrow, has_down, above)

    def unpack_body(t, carry):
        src = pl.ds(pl.multiple_of(8 * t, 8), 8)
        dst = pl.ds(pl.multiple_of(OFF - HALO + 8 * t, 8), 8)
        rowmask = inside_rows(OFF - HALO + 8 * t, sub)
        from_left = crecv[0, src, :] * (rowmask * has_left)
        from_right = crecv[1, src, :] * (rowmask * has_right)
        odd = (lane // HALO) % 2 == 1
        merged = (jnp.where(odd, from_left, from_right), jnp.where(odd, from_right, from_left))
        for k in range(12):
            moved = pltpu.roll(merged[k % 2], (-HALO * k) % LANES, axis=1) if k else merged[0]
            tile = jnp.where(edge_lanes, moved, 0.0)
            if k < 8:
                rbuf[nu, k, dst, :] = tile
            else:
                cbuf[k - 8, nu, dst, :] = tile
        return carry

    def sunpack_body(t, carry):
        src = pl.ds(pl.multiple_of(16 * t, 16), 16)
        rowmask = inside_rows(16 * t, lax.broadcasted_iota(jnp.int32, (16, LANES), 0))
        for part in range(2):
            cols = slice(part * LANES, (part + 1) * LANES)
            from_left = srecv[0, src, cols].astype(jnp.float32) * (rowmask * has_left)
            from_right = srecv[1, src, cols].astype(jnp.float32) * (rowmask * has_right)
            odd = (lane16 // HALO) % 2 == 1
            merged = (jnp.where(odd, from_left, from_right), jnp.where(odd, from_right, from_left))
            for k in range(16 if part == 0 else 9):
                moved = pltpu.roll(merged[k % 2], (-HALO * k) % LANES, axis=1) if k else merged[0]
                sfull[nu, 16 * part + k, src, :] = jnp.where(edge_lanes16, moved, 0.0)
        return carry

    colmask = [jnp.ones((8, LANES), jnp.float32)] * nu + [
        jnp.where(lane < LANES // 2, has_right, has_left)]

    def sym_tile(at, rotated):
        here = pl.ds(at, 8)
        rowmask = inside_rows(at, sub) * 0.5
        masks = {b: ring_shifts([m * rowmask for m in colmask], -b, lane) for b in range(-2, 3)}
        for o, (a, b) in enumerate(OFFSETS):
            if b == 0:
                own = [sfull[u, o, here, :] for u in range(nt)]
            else:
                rolled = [
                    symp[u, o, here, :] if rotated and u < nu else pltpu.roll(sfull[u, o, here, :], b % LANES, axis=1)
                    for u in range(nt)]
                if b < 0:
                    own = [jnp.where(lane < LANES + b, rolled[u], rolled[(u + 1) % nt]) for u in range(nt)]
                else:
                    own = [jnp.where(lane >= b, rolled[u], rolled[(u - 1) % nt]) for u in range(nt)]
            for u in range(nt):
                mirror = sfull[u, 24 - o, pl.ds(at + a, 8), :]
                symp[u, o, here, :] = (own[u] + mirror) * masks[b][u]

    inner_tiles = nrow // 8 - 2
    inner_at = lambda t: pl.multiple_of(OFF + 8 + 8 * t, 8)
    rim_at = lambda t: pl.multiple_of(OFF - HALO + 8 * t + (t // 2) * 8 * inner_tiles, 8)
    edge_at = lambda t: pl.multiple_of(OFF + t * (nrow - 8), 8)
    halo_at = lambda t: pl.multiple_of(OFF - HALO + t * (nrow + HALO), 8)

    def each(count, place, body):
        def step(t, carry):
            body(place(t))
            return carry
        lax.fori_loop(0, count, step, 0)

    def lap_tile(at):
        here = pl.ds(at, 8)
        above, below = pl.ds(at - 1, 8), pl.ds(at + 1, 8)
        tiles = lambda k, rows: [cbuf[k, u, rows, :] for u in range(nt)]
        kap, con, inv, msk = (tiles(k, here) for k in range(4))
        con_n = ring_shifts(con, 1, lane)
        east = [0.5 * (con[u] + con_n[u]) for u in range(nt)]
        west = ring_shifts(east, -1, lane)
        inv_e, inv_w = ring_shifts(inv, 1, lane), ring_shifts(inv, -1, lane)
        msk_e, msk_w = ring_shifts(msk, 1, lane), ring_shifts(msk, -1, lane)
        for u in range(nt):
            north = 0.5 * (con[u] + cbuf[1, u, above, :])
            south = 0.5 * (con[u] + cbuf[1, u, below, :])
            diag = kap[u] + north + south + west[u] + east[u]
            lap[0, u, here, :] = inv[u] * diag * msk[u]
            lap[1, u, here, :] = inv[u] * north * cbuf[3, u, above, :]
            lap[2, u, here, :] = inv[u] * south * cbuf[3, u, below, :]
            lap[3, u, here, :] = inv_w[u] * west[u] * msk[u]
            lap[4, u, here, :] = inv_e[u] * east[u] * msk[u]
            lap[5, u, here, :] = msk[u] * diag
            lap[6, u, here, :] = msk[u] * north
            lap[7, u, here, :] = msk[u] * south
            lap[8, u, here, :] = msk_w[u] * west[u]
            lap[9, u, here, :] = msk_e[u] * east[u]
            lap[10, u, here, :] = 1.0 - msk[u]
            if u < nu:
                lap[11, u, here, :] = 1.0 / inv[u]

    def apply_m(src, dst, place, count):
        def body(at):
            for p0 in range(0, PROBES, 2):
                pair_p = (p0, p0 + 1)
                field = {(p, a, u): src[u, p, pl.ds(at + a, 8), :] for p in pair_p for a in range(-2, 3) for u in range(nt)}
                total = {}
                for b in range(-2, 3):
                    part = {}
                    for a in range(-2, 3):
                        o = (a + 2) * 5 + b + 2
                        for u in range(nt):
                            weight = symp[u, o, pl.ds(at, 8), :]
                            for p in pair_p:
                                term = weight * field[p, a, u]
                                part[p, u] = term if a == -2 else part[p, u] + term
                    for p in pair_p:
                        moved = ring_shifts([part[p, u] for u in range(nt)], b, lane)
                        for u in range(nt):
                            total[p, u] = moved[u] if b == -2 else total[p, u] + moved[u]
                for p in pair_p:
                    for u in range(nt):
                        dst[u, p, pl.ds(at, 8), :] = total[p, u]
        each(count, place, body)

    def half_laplace(first, src, at, p, coefs):
        centre = [src[u, p, pl.ds(at, 8), :] for u in range(nt)]
        to_east = ring_shifts([coefs[3][u] * centre[u] for u in range(nt)], 1, lane)
        to_west = ring_shifts([coefs[4][u] * centre[u] for u in range(nt)], -1, lane)
        out = []
        for u in range(nt):
            across = to_east[u] + to_west[u]
            along = coefs[1][u] * src[u, p, pl.ds(at - 1, 8), :] + coefs[2][u] * src[u, p, pl.ds(at + 1, 8), :]
            out.append(coefs[0][u] * centre[u] - (across + along))
        return out

    def inner_a(src, start, count):
        def body(t, carry):
            at = start + 8 * t
            coefs = [[lap[k, u, pl.ds(at, 8), :] for u in range(nt)] for k in range(5)]
            for p in range(PROBES):
                out = half_laplace(0, src, at, p, coefs)
                for u in range(nt):
                    tbuf[u, p, pl.ds(at, 8), :] = out[u]
            return carry
        lax.fori_loop(0, count, body, 0)

    def outer_a(src, dst, start, count, keep):
        def body(t, carry):
            at = start + 8 * t
            coefs = [[lap[5 + k, u, pl.ds(at, 8), :] for u in range(nt)] for k in range(6)]
            for p in range(PROBES):
                out = half_laplace(5, tbuf, at, p, coefs)
                for u in range(keep):
                    dst[u, p, pl.ds(at, 8), :] = out[u] + coefs[5][u] * src[u, p, pl.ds(at, 8), :]
            return carry
        lax.fori_loop(0, count, body, 0)

    pairs = [(k, l) for k in range(8) for l in range(k, 8)]

    groups = -(-len(pairs) // 8)

    def gram(terms):
        def body(i, acc):
            u = i // (nrow // 8)
            rows = pl.ds(pl.multiple_of(OFF + 8 * (i % (nrow // 8)), 8), 8)
            for first, second, weight in terms:
                a = [first[u, p, rows, :] for p in range(PROBES)]
                if weight is not None:
                    w = lap[weight, u, rows, :]
                    a = [w * x for x in a]
                b = [second[u, p, rows, :] for p in range(PROBES)]
                acc = tuple(acc[n] + a[k] * b[l] for n, (k, l) in enumerate(pairs))
            return acc
        start = tuple(jnp.zeros((8, LANES), jnp.float32) for _ in pairs)
        return lax.fori_loop(0, nu * (nrow // 8), body, start, unroll=2)

    def to_lanes(total, first, acc):
        for j in range(groups):
            stacked = None
            for s in range(8):
                if 8 * j + s < len(acc):
                    entry = jnp.broadcast_to(jnp.sum(acc[8 * j + s], axis=0, keepdims=True), (8, LANES))
                    stacked = entry if stacked is None else jnp.where(sub == s, entry, stacked)
            total = jnp.where(lane == first + j, jnp.sum(stacked, axis=1, keepdims=True), total)
        return total

    def one_row(total):
        spread = pltpu.roll(total, 0, axis=1, stride=16, stride_axis=0)
        return jnp.sum(spread, axis=0, keepdims=True)

    def entries(line, first):
        out = [[None] * 8 for _ in range(8)]
        for n, (k, l) in enumerate(pairs):
            at = 16 * (n % 8) + first + n // 8
            out[k][l] = out[l][k] = jnp.broadcast_to(line[:, at : at + 1], (8, LANES))
        return out

    def entry_rows(spread):
        out = []
        for k in range(8):
            line = spread[k][0]
            for l in range(1, 8):
                line = jnp.where(lane == l, spread[k][l], line)
            out.append(line)
        return out

    def post(step, phase, value):
        mine, partners, count = ((mine1, partners1, group1), (pair, partners2, group2))[phase]
        buf = grams.at[step, phase]
        buf[mine] = value
        copies = [pltpu.make_async_remote_copy(
            src_ref=buf.at[mine], dst_ref=buf.at[mine],
            send_sem=gsend.at[step, phase, d], recv_sem=grecv.at[step, phase, mine],
            device_id=who, device_id_type=MESH) for d, who in enumerate(partners)]
        for copy in copies:
            copy.start()

        def finish():
            for d in range(1, count):
                slot = (mine + d) % count
                pltpu.make_async_copy(buf.at[slot], buf.at[slot], grecv.at[step, phase, slot]).wait()
            terms = [buf[k] for k in range(count)]
            while len(terms) > 1:
                terms = [terms[i] + terms[i + 1] for i in range(0, len(terms) - 1, 2)] + terms[len(terms) & ~1 :]
            pending.extend(copies)
            return terms[0]
        return finish

    pending = []
    zeros = jnp.zeros((8, LANES), jnp.float32)

    for copy in direct:
        copy.wait_recv()
    lax.fori_loop(1, nrow // 8 + 1, unpack_body, 0)
    each(inner_tiles, inner_at, lap_tile)
    lax.fori_loop(1, nrow // 16 + 1, sunpack_body, 0)
    each(inner_tiles, inner_at, lambda at: sym_tile(at, True))
    apply_m(rbuf, zbuf, inner_at, inner_tiles)
    for copy in row_copies:
        copy.wait_recv()
    for side, keep, at in ((0, has_up, OFF - HALO), (1, has_down, OFF + nrow)):
        for u in range(nu):
            cols = slice(u * LANES, (u + 1) * LANES)
            for k in range(12):
                item = fland[side, k, :, cols] * keep
                if k < 8:
                    rbuf[u, k, at : at + 8, :] = item
                else:
                    cbuf[k - 8, u, at : at + 8, :] = item
            for j in range(13):
                both = sland[side, j, :, cols].astype(jnp.float32) * keep
                sfull[u, 2 * j, at : at + 8, :] = both[0:8]
                if j < 12:
                    sfull[u, 2 * j + 1, at : at + 8, :] = both[8:16]

    for copy in corners:
        copy.wait_recv()
    lax.fori_loop(0, 2, lambda t, carry: unpack_body(t * (nrow // 8 + 1), carry), 0)
    lax.fori_loop(0, 2, lambda t, carry: sunpack_body(t * (nrow // 16 + 1), carry), 0)
    each(4, rim_at, lap_tile)
    each(2, edge_at, lambda at: sym_tile(at, True))
    each(2, halo_at, lambda at: sym_tile(at, False))
    apply_m(rbuf, zbuf, rim_at, 4)
    inner_a(zbuf, OFF - 8, (nrow + 16) // 8)
    outer_a(zbuf, wbuf, OFF - 4, (nrow + 8) // 8, nt)
    total = to_lanes(zeros, 0, gram([(rbuf, zbuf, None)]))
    total = to_lanes(total, groups, gram([(zbuf, wbuf, None)]))
    step0 = post(0, 0, one_row(total))
    apply_m(wbuf, ybuf, lambda t: OFF - 2 + 8 * t, (nrow + 8) // 8)
    step1 = post(1, 0, one_row(to_lanes(zeros, 0, gram([(wbuf, ybuf, None)]))))
    step0 = post(0, 1, step0())
    inner_a(ybuf, OFF - 1, (nrow + 8) // 8)
    step2 = post(2, 0, one_row(to_lanes(zeros, 0, gram([(tbuf, tbuf, 11), (ybuf, ybuf, 10)]))))

    outer_a(ybuf, vbuf, OFF, nrow // 8, nu)
    add = lambda x, y: [a + b for a, b in zip(x, y)]
    minus = lambda x, y: [a - b for a, b in zip(x, y)]

    def keep_coef(m, rows):
        spread = splats(stack_rows(rows, sub), 0)
        for k in range(8):
            for l in range(8):
                coef[m, l, k] = spread[k][l]
        return spread

    def mix(jobs, l0, at_t, u, rows, cols):
        for field, m, base, sign, target in jobs:
            f = [field(k, u, rows, cols) for k in range(8)]
            for l in (l0, l0 + 1):
                total = coef[m, l, 0] * f[0]
                for k in range(1, 8):
                    total = total + coef[m, l, k] * f[k]
                if base is not None:
                    old = base(l, u, rows, cols)
                    total = old + total if sign > 0 else old - total
                elif sign < 0:
                    total = -total
                target[l, at_t, cols] = total

    ext = lambda ref: lambda k, u, rows, cols: ref[u, k, pl.ds(pl.multiple_of(rows + OFF, 8), 8), :]
    flat = lambda ref: lambda k, u, rows, cols: ref[k, pl.ds(pl.multiple_of(rows, 8), 8), cols]

    def mix_all(jobs, l0):
        def body(t, carry):
            for u in range(nu):
                mix(jobs, l0, pl.ds(pl.multiple_of(8 * t, 8), 8), u, 8 * t, slice(u * LANES, (u + 1) * LANES))
            return carry
        lax.fori_loop(0, nrow // 8, body, 0)

    step1 = post(1, 1, step1())
    line0 = step0()
    g1s, g2s = entries(line0, 0), entries(line0, groups)
    g1r, g2r = entry_rows(g1s), entry_rows(g2s)
    alpha = substitute(factor(g2s), g1r)
    alpha_s = keep_coef(0, alpha)
    step2 = post(2, 1, step2())
    for l0 in range(0, PROBES, 2):
        mix_all([(ext(zbuf), 0, None, 1, xs), (ext(wbuf), 0, ext(rbuf), -1, rs),
                 (ext(ybuf), 0, None, -1, ps), (ext(vbuf), 0, None, -1, ws)], l0)
    fact1 = factor(g1s)
    g3s = entries(step1(), 0)
    g3_alpha = product(g3s, alpha)
    gamma = minus(minus(g1r, product(g2s, alpha)), product_t(alpha_s, minus(g2r, g3_alpha)))
    beta = substitute(fact1, gamma)
    eye = [jnp.where(lane == k, 1.0, 0.0) for k in range(8)]
    b_rows = add(beta, eye)
    b_s = keep_coef(1, b_rows)
    part = product_t(b_s, minus(product(g2s, b_rows), g3_alpha))
    g3_b = product(g3s, b_rows)
    for l0 in range(0, PROBES, 2):
        mix_all([(ext(zbuf), 1, flat(ps), 1, ps), (ext(wbuf), 1, flat(ws), 1, ws)], l0)

    g4s = entries(step2(), 0)
    curv = minus(part, product_t(alpha_s, minus(g3_b, product(g4s, alpha))))
    curv_s = splats(stack_rows(curv, sub), 0)
    curv_s = [[0.5 * (curv_s[k][l] + curv_s[l][k]) for l in range(8)] for k in range(8)]
    keep_coef(2, substitute(factor(curv_s), gamma))

    for l0 in range(0, PROBES, 2):
        mix_all([(flat(ps), 2, flat(xs), 1, xs), (flat(ws), 2, flat(rs), -1, rs)], l0)
    for copy in pending + col_copies + row_copies:
        copy.wait_send()


def copy_kernel(x_in, r_in, x_out, r_out, sem):
    copies = []
    for p in range(0, PROBES, 2):
        two = pl.ds(p, 2)
        copies.append(pltpu.make_async_copy(x_in.at[two], x_out.at[two], sem.at[p]))
        copies.append(pltpu.make_async_copy(r_in.at[two], r_out.at[two], sem.at[p + 1]))
    for copy in copies:
        copy.start()
    for copy in copies:
        copy.wait()


def shards(probes, kappa_sq, conduct, inv_mass, spai, sea_mask):
    _, nrow, ncol = probes.shape
    rows_n, cols_n = lax.axis_size("row"), lax.axis_size("col")
    nu = ncol // LANES
    nt = nu + 1
    ext = nrow + 2 * OFF
    most = max(2 * cols_n, rows_n // 2)
    f32, bf16 = jnp.float32, jnp.bfloat16
    field = pltpu.VMEM((nt, PROBES, ext, LANES), f32)
    dma = pltpu.SemaphoreType.DMA
    scratch = [
        field, field, field, field, field,
        pltpu.VMEM((25, nrow, ncol), bf16),
        pltpu.VMEM((nt, 25, ext, LANES), f32),
        pltpu.VMEM((nt, 25, ext, LANES), f32),
        pltpu.VMEM((4, nt, ext, LANES), f32),
        pltpu.VMEM((12, nt, ext, LANES), f32),
        pltpu.VMEM((2, 12, HALO, ncol), f32),
        pltpu.VMEM((2, 13, 2 * HALO, ncol), bf16),
        pltpu.VMEM((2, 12, HALO, ncol), f32),
        pltpu.VMEM((2, 13, 2 * HALO, ncol), bf16),
        pltpu.VMEM((nrow, ncol), jnp.int32),
        pltpu.VMEM((2, nrow, LANES), f32),
        pltpu.VMEM((2, nrow, 2 * LANES), bf16),
        pltpu.VMEM((2, nrow + 2 * HALO, LANES), f32),
        pltpu.VMEM((2, ext, 2 * LANES), bf16),
        pltpu.VMEM((3, 2, most, 1, LANES), f32),
        pltpu.VMEM((3, 8, 8, 8, LANES), f32),
        pltpu.VMEM((PROBES, nrow, ncol), f32),
        pltpu.VMEM((PROBES, nrow, ncol), f32),
        field,
        dma((2 + 4 * nu,)),
        dma((16,)), dma((16,)),
        dma((3, 2, most)), dma((3, 2, most)),
    ]
    out = jax.ShapeDtypeStruct(probes.shape, f32)
    hbm = pl.BlockSpec(memory_space=pl.ANY)
    parts = pl.pallas_call(
        functools.partial(kernel, nrow, ncol, rows_n, cols_n),
        out_shape=(pltpu.VMEM(probes.shape, f32),) * 2,
        in_specs=[pl.BlockSpec(memory_space=pltpu.HBM)] * 6,
        out_specs=(pl.BlockSpec(memory_space=pltpu.VMEM),) * 2,
        scratch_shapes=scratch,
        compiler_params=pltpu.CompilerParams(
            collective_id=0, has_side_effects=True, vmem_limit_bytes=48 * 1024 * 1024),
    )(*[pltpu.with_memory_space_constraint(v, pltpu.HBM) for v in (probes, kappa_sq, conduct, inv_mass, spai, sea_mask)])
    return pl.pallas_call(
        copy_kernel,
        out_shape=(out, out),
        in_specs=[hbm] * 2,
        out_specs=(pl.BlockSpec(memory_space=pltpu.HBM),) * 2,
        scratch_shapes=[dma((8,))],
        compiler_params=pltpu.CompilerParams(vmem_limit_bytes=16 * 1024 * 1024),
    )(*parts)


def solution(mesh):
    field = P(None, "row", "col")
    cell = P("row", "col")
    return jax.shard_map(
        shards, mesh=mesh, in_specs=(field, cell, cell, cell, field, cell),
        out_specs=(field, field), check_vma=False)
```
